128 devices in a mesh: ctx: 32 (over z, x_lo, y), ep: 4 (over x_hi, core).
Axes of the slice: x: 4 (x_hi: 2, x_lo: 2; x = x_hi * 2 + x_lo), y: 4, z: 4, core: 2. Of those that a mesh axis runs over, the one named last changes fastest.
Arguments:
- inputs: bfloat16 [2, 8192, 1536], P(None, ('ctx', 'ep')), may hold values from -6 to 6
- cotangent: bfloat16 [2, 8192, 1536], P(None, ('ctx', 'ep')), may hold values from -6 to 6
- segments: int32 [2, 8192], P(None, 'ctx'), may hold values from 0 to 8, as said below
- routes: int32 [2, 8192, 8], P(None, ('ctx', 'ep')), may hold values from 0 to 11, all different within a row; in each aligned block of 64 rows (0 to 63, 64 to 127, ..., all dimensions but the last counted through in order) at most 48 rows name the same one
- attn_gain: bfloat16 [1536], P(('ctx', 'ep')), may hold values from 0.5 to 1.5
- w_query: bfloat16 [1536, 1536], P('ctx', 'ep'), may hold values from -0.15625 to 0.15625
- key_weight: bfloat16 [1536, 512], P('ctx', 'ep'), may hold values from -0.15625 to 0.15625
- value_weight: bfloat16 [1536, 512], P('ctx', 'ep'), may hold values from -0.15625 to 0.15625
- w_out: bfloat16 [1536, 1536], P('ep', 'ctx'), may hold values from -6 to 6
- ffn_gain: bfloat16 [1536], P(('ctx', 'ep')), may hold values from 0.5 to 1.5
- router: bfloat16 [1536, 12], P(('ctx', 'ep')), may hold values from -0.078125 to 0.078125
- w_gate: bfloat16 [12, 1536, 512], P('ep', 'ctx'), may hold values from -0.15625 to 0.15625
- w_up: bfloat16 [12, 1536, 512], P('ep', 'ctx'), may hold values from -0.15625 to 0.15625
- w_down: bfloat16 [12, 512, 1536], P('ep', None, 'ctx'), may hold values from -1 to 1
Outputs:
- outputs: bfloat16 [2, 8192, 1536], P(None, ('ctx', 'ep'))
- input_grad: bfloat16 [2, 8192, 1536], P(None, ('ctx', 'ep'))
- grad_attn_gain: float32 [1536], P(('ctx', 'ep'))
- grad_query: float32 [1536, 1536], P('ctx', 'ep')
- grad_key: float32 [1536, 512], P('ctx', 'ep')
- grad_value: float32 [1536, 512], P('ctx', 'ep')
- grad_out: float32 [1536, 1536], P('ep', 'ctx')
- grad_ffn_gain: float32 [1536], P(('ctx', 'ep'))
- grad_router: float32 [1536, 12], P(('ctx', 'ep'))
- grad_gate: float32 [12, 1536, 512], P('ep', 'ctx')
- grad_up: float32 [12, 1536, 512], P('ep', 'ctx')
- grad_down: float32 [12, 512, 1536], P('ep', None, 'ctx')
The draws below stay inside these ranges and needn't reach their ends.
Inputs may be any that keep to these rules, and one draw needn't show every extreme that they name: `segments`: never falls along a micro-batch; document 4 starts within the first 256 tokens and ends within the last 256 tokens. `routes`: each token names 8 different experts; within one micro-batch, among the tokens of one device no expert is named more than 48 times.
All inputs are finite; a program needn't handle non-finite values.
Results may differ from the reference program's by a relative error of at most 0.034.
Values may be sent and summed in bfloat16 or wider, within the bound.
No kernel may reach another device: no remote copies, remote signals or barrier semaphores. Data moves between devices by JAX's collectives and lax.ppermute only.
A program may use at most 128 MiB of HBM per device.

```python
import math
from functools import partial
import jax
import jax.numpy as jnp
import numpy as np
from jax import lax

MODEL_DIM = 1536
QUERY_HEADS = 24
KEY_VALUE_HEADS = 8
HEAD_DIM = 64
FF = 512
TOP = 8
MB = 2
TOK_DEV = 64
CTX_TOK = 256
SEQ = 8192
EXPERTS = 12
CAP = 48


def draw_segments(key, part):
    key = jax.random.fold_in(key, 7)
    head_key, tail_key = jax.random.split(key)
    head_draw = jax.random.randint(head_key, (MB, 4), 0, CTX_TOK)
    tail_draw = jax.random.randint(tail_key, (MB, 4), 0, CTX_TOK)
    head_cuts = 1 + head_draw * head_draw // CTX_TOK
    tail_cuts = SEQ - 1 - tail_draw * tail_draw // CTX_TOK
    cut_points = jnp.concatenate([head_cuts, tail_cuts], axis=1)
    positions = jnp.arange(SEQ, dtype=jnp.int32)
    passed = (cut_points[:, None, :] <= positions[None, :, None]).astype(jnp.int32)
    return jnp.sum(passed, axis=-1).astype(jnp.int32)


def levels(stream_key, extent, cuts, smallest, largest):
    def one(axis_at, blocks):
        draws = jax.random.uniform(jax.random.fold_in(jax.random.fold_in(stream_key, 6), axis_at), (blocks,), jnp.float32, smallest / len(cuts), largest / len(cuts))
        return jnp.repeat(jnp.exp(draws), extent[axis_at] // blocks).reshape((-1,) + (1,) * (len(extent) - axis_at - 1))

    level = one(*cuts[0])
    for cut in cuts[1:]:
        level = level * one(*cut)
    return level


def routed_block(stream_key, own, number, rows, amount, top, bound, lean):
    order = jax.random.permutation(stream_key, amount)
    crowded, usual = load_shares(amount, rows * top, bound, lean, True), load_shares(amount, rows * top, bound, lean, False)
    places = jnp.arange(amount)

    def named(sizes, offset_by):
        used = int((sizes > 0).sum())
        fixed = max(1, used // 4)
        shifted = fixed + (places - fixed + offset_by * (used - fixed)) % max(1, amount - fixed)
        return jnp.zeros((amount,), jnp.int32).at[order[jnp.where(places < fixed, places, shifted)]].set(jnp.asarray(sizes, jnp.int32))

    sizes = jnp.where(number % 4 == 0, named(crowded, number // 4), named(usual, number - number // 4 - 1))
    mixed = jax.random.permutation(jax.random.fold_in(own, 3), amount)
    giver, sink = mixed[0:amount // 2 * 2:2], mixed[1:amount // 2 * 2:2]
    margin = jnp.minimum(sizes[giver] - 1, bound - sizes[sink]) // 2
    margin = jnp.where((giver == order[0]) | (sink == order[0]) | (sizes[sink] == 0), 0, jnp.maximum(margin, 0))
    shifted = jax.random.randint(jax.random.fold_in(own, 4), (amount // 2,), 0, 1 << 20) % (margin + 1)
    sizes = sizes.at[giver].add(-shifted).at[sink].add(shifted)
    items = jnp.searchsorted(jnp.cumsum(sizes), jnp.arange(rows * top), side="right").astype(jnp.int32)
    grid = items.reshape(top, rows).T
    grid = grid[jax.random.permutation(jax.random.fold_in(own, 1), rows)]
    offset_by = jax.random.randint(jax.random.fold_in(own, 2), (rows, 1), 0, top)
    return jnp.take_along_axis(grid, (jnp.arange(top)[None, :] + offset_by) % top, axis=1)


def load_shares(amount, total, bound, slope, full):
    portions = [(1 << 20) // math.isqrt(rank ** slope) + 1 for rank in range(1, amount + 1)]
    largest = bound if full else min(bound, max(-(-total // amount), total * portions[0] // sum(portions)))
    least = 1 if total - largest >= amount - 1 else 0
    given, surplus = [largest] + [least] * (amount - 1), total - largest - least * (amount - 1)
    while surplus > 0:
        candidates = [i for i in range(1, amount) if given[i] < largest] or [i for i in range(1, amount) if given[i] < bound]
        mass, budget = sum([portions[i] for i in candidates]), surplus
        for i in candidates:
            addition = min(bound - given[i], max(1, budget * portions[i] // mass), surplus)
            given[i] = given[i] + addition
            surplus = surplus - addition
    return np.array(given)


def bell_draw(key, extent, width, limit, cuts=(), held_as=jnp.bfloat16):
    entries = width * jax.random.normal(key, extent, jnp.float32)
    if cuts:
        entries = entries * levels(key, extent, cuts, -0.22, 0.18)
    return jnp.clip(entries, -limit, limit).astype(held_as)


def setup_inputs(seed: int = 0) -> dict:
    key_list = jax.random.split(jax.random.key(seed), 15)
    inputs = bell_draw(key_list[0], (MB, SEQ, MODEL_DIM), 1.0, 6.0, ((1, 128),))
    cotangent = bell_draw(key_list[1], (MB, SEQ, MODEL_DIM), 1.0, 6.0, ((1, 128),))
    segments = draw_segments(jax.random.fold_in(key_list[14], 71), 0)
    routes_keys = jax.random.split(jax.random.fold_in(key_list[3], 1), MB * SEQ // TOK_DEV)
    routes_turns = jax.random.permutation(jax.random.fold_in(key_list[3], 3), MB * SEQ // TOK_DEV)
    routes = jax.vmap(lambda own, number: routed_block(jax.random.fold_in(key_list[3], 2), own, number, TOK_DEV, EXPERTS, TOP, CAP, 1))(routes_keys, routes_turns).reshape((MB, SEQ, TOP))
    attn_gain = jnp.clip(1.0 + 0.1 * jax.random.normal(key_list[4], (MODEL_DIM,), jnp.float32), 0.5, 1.5).astype(jnp.bfloat16)
    w_query = bell_draw(key_list[5], (MODEL_DIM, QUERY_HEADS * HEAD_DIM), MODEL_DIM ** -0.5, 0.15625, ((0, 32), (1, 4)))
    key_weight = bell_draw(key_list[6], (MODEL_DIM, KEY_VALUE_HEADS * HEAD_DIM), MODEL_DIM ** -0.5, 0.15625, ((0, 32), (1, 4)))
    value_weight = bell_draw(key_list[7], (MODEL_DIM, KEY_VALUE_HEADS * HEAD_DIM), MODEL_DIM ** -0.5, 0.15625, ((0, 32), (1, 4)))
    w_out = bell_draw(key_list[8], (QUERY_HEADS * HEAD_DIM, MODEL_DIM), 1.0, 6.0, ((0, 4), (1, 32)))
    ffn_gain = jnp.clip(1.0 + 0.1 * jax.random.normal(key_list[9], (MODEL_DIM,), jnp.float32), 0.5, 1.5).astype(jnp.bfloat16)
    router = bell_draw(key_list[10], (MODEL_DIM, EXPERTS), (4 * MODEL_DIM) ** -0.5, 0.078125, ((0, 128),))
    w_gate = bell_draw(key_list[11], (EXPERTS, MODEL_DIM, FF), MODEL_DIM ** -0.5, 0.15625, ((0, 4), (1, 32)))
    w_up = bell_draw(key_list[12], (EXPERTS, MODEL_DIM, FF), MODEL_DIM ** -0.5, 0.15625, ((0, 4), (1, 32)))
    w_down = bell_draw(key_list[13], (EXPERTS, FF, MODEL_DIM), (FF // 16) ** -0.5, 1.0, ((0, 4), (2, 32)))
    return dict(inputs=inputs, cotangent=cotangent, segments=segments, routes=routes, attn_gain=attn_gain, w_query=w_query, key_weight=key_weight, value_weight=value_weight, w_out=w_out, ffn_gain=ffn_gain, router=router, w_gate=w_gate, w_up=w_up, w_down=w_down)


EPSILON = 1e-06
MASKED = -1e+30

@jax.custom_vjp
def reduced_precision(v):
    return lax.optimization_barrier(v.astype(jnp.bfloat16)).astype(jnp.float32)

@jax.custom_vjp
def reduced_backward(v):
    return v

def low_keep(v):
    return (reduced_precision(v), None)

def low_pass(kept, grad):
    return (grad,)

def back_keep(v):
    return (v, None)

def back_low(kept, grad):
    return (reduced_precision(grad),)
reduced_precision.defvjp(low_keep, low_pass)
reduced_backward.defvjp(back_keep, back_low)

def precise_product(left, right):
    return jnp.dot(left, right, precision=lax.Precision.HIGHEST)

def rms_scale(values):
    return lax.rsqrt(lax.optimization_barrier(jnp.mean(values * values, axis=-1, keepdims=True)) + EPSILON)

def rope_tables(positions, head_width):
    half_width = head_width // 2
    inverse = jnp.exp(jnp.arange(half_width, dtype=jnp.float32) * (-2.0 * math.log(10000.0) / head_width))
    angles = positions.astype(jnp.float32)[:, None] * inverse[None, :]
    return (jnp.cos(angles)[:, None, :], jnp.sin(angles)[:, None, :])

def apply_rotation(values, cosine_table, sine_values):
    half_width = values.shape[-1] // 2
    lead_half = values[..., :half_width]
    tail_half = values[..., half_width:]
    return jnp.concatenate([lead_half * cosine_table - tail_half * sine_values, tail_half * cosine_table + lead_half * sine_values], axis=-1)

def layer_forward(inputs, gain_one, w_query, key_weight, value_weight, w_out, gain_two, router, w_gate, w_up, w_down, segs, chosen_ids):
    sequence_length = inputs.shape[0]
    normalized_input = reduced_precision(inputs * rms_scale(inputs) * gain_one)
    positions = jnp.arange(sequence_length, dtype=jnp.int32)
    cosine_table, sine_values = rope_tables(positions, HEAD_DIM)
    query_matrix = reduced_precision(apply_rotation(reduced_backward(precise_product(normalized_input, w_query)).reshape(sequence_length, QUERY_HEADS, HEAD_DIM), cosine_table, sine_values))
    key_matrix = reduced_precision(apply_rotation(reduced_backward(precise_product(normalized_input, key_weight)).reshape(sequence_length, KEY_VALUE_HEADS, HEAD_DIM), cosine_table, sine_values))
    value_matrix = reduced_precision(reduced_backward(precise_product(normalized_input, value_weight))).reshape(sequence_length, KEY_VALUE_HEADS, HEAD_DIM)
    heads_per_group = QUERY_HEADS // KEY_VALUE_HEADS
    rows_per_block = min(256, sequence_length)
    count_of_blocks = sequence_length // rows_per_block
    score_scale = 1.0 / math.sqrt(HEAD_DIM)

    def attend(pieces):
        q_blk, q_pos, q_seg = pieces
        raw_scores = jnp.einsum('qhgd,khd->hgqk', q_blk, key_matrix, precision=lax.Precision.HIGHEST)
        scores = reduced_backward(raw_scores) * score_scale
        allowed = (q_seg[:, None] == segs[None, :]) & (positions[None, :] <= q_pos[:, None])
        scores = jnp.where(allowed, scores, MASKED)
        row_max = lax.optimization_barrier(jnp.max(scores, axis=-1, keepdims=True))
        log_total = row_max + jnp.log(lax.optimization_barrier(jnp.sum(jnp.exp(scores - row_max), axis=-1, keepdims=True)))
        probabilities = reduced_precision(jnp.exp(scores - log_total))
        mixed_blk = jnp.einsum('hgqk,khd->qhgd', probabilities, value_matrix, precision=lax.Precision.HIGHEST)
        return mixed_blk.reshape(rows_per_block, QUERY_HEADS * HEAD_DIM)
    query_blocks = query_matrix.reshape(count_of_blocks, rows_per_block, KEY_VALUE_HEADS, heads_per_group, HEAD_DIM)
    mixed = lax.map(jax.checkpoint(attend), (query_blocks, positions.reshape(count_of_blocks, rows_per_block), segs.reshape(count_of_blocks, rows_per_block)))
    mixed = reduced_precision(reduced_backward(mixed.reshape(sequence_length, QUERY_HEADS * HEAD_DIM)))
    residual = inputs + reduced_backward(precise_product(mixed, w_out))
    tokens = reduced_precision(residual * rms_scale(residual) * gain_two)
    logits = reduced_backward(precise_product(tokens, router))
    chosen = jnp.any(chosen_ids[:, :, None] == jnp.arange(EXPERTS, dtype=jnp.int32)[None, None, :], axis=1)
    gate_probs = jax.nn.softmax(jnp.where(chosen, logits, MASKED), axis=-1)

    def expert(running, pieces):
        gate_mat, up_mat, down_mat, gate_column = pieces
        expert_in = reduced_backward(tokens)
        gate_pre = reduced_backward(precise_product(expert_in, gate_mat))
        up_pre = reduced_backward(precise_product(expert_in, up_mat))
        hidden = reduced_precision(jax.nn.silu(gate_pre) * up_pre)
        expert_out = reduced_precision(reduced_backward(precise_product(hidden, down_mat)))
        return (running + gate_column[:, None] * expert_out, None)
    combined, unused = lax.scan(jax.checkpoint(expert), jnp.zeros_like(residual), (w_gate, w_up, w_down, gate_probs.T))
    return residual + combined

def reference(inputs, cotangent, segments, routes, attn_gain, w_query, key_weight, value_weight, w_out, ffn_gain, router, w_gate, w_up, w_down):
    params = [p.astype(jnp.float32) for p in (attn_gain, w_query, key_weight, value_weight, w_out, ffn_gain, router, w_gate, w_up, w_down)]
    outputs = []
    input_grads = []
    totals = [jnp.zeros_like(p) for p in params]
    for micro_batch in range(MB):
        forward = partial(layer_forward, segs=segments[micro_batch], chosen_ids=routes[micro_batch])
        result, pullback = jax.vjp(forward, inputs[micro_batch].astype(jnp.float32), *params)
        gradients = pullback(cotangent[micro_batch].astype(jnp.float32))
        outputs.append(result.astype(jnp.bfloat16))
        input_grads.append(gradients[0].astype(jnp.bfloat16))
        totals = [running + new_grad for running, new_grad in zip(totals, gradients[1:])]
    return (jnp.stack(outputs), jnp.stack(input_grads), totals[0], totals[1], totals[2], totals[3], totals[4], totals[5], totals[6], totals[7], totals[8], totals[9])
```

```python
import math

import jax
import jax.numpy as jnp
from jax import lax
from jax.experimental import pallas as pl
from jax.experimental.pallas import tpu as pltpu
from jax.sharding import PartitionSpec as P

HEAD_DIM = 64
HALF = 32
GROUP = 3
KV_DEV = 2
EXP_DEV = 3
EXPERTS = 12
MB = 2
COMBOS = MB * KV_DEV
BLOCK = 256
LANES = GROUP * BLOCK
COVERING = 4.0
EPSILON = 1e-06
MASKED = -1e30
F32 = jnp.float32
BF16 = jnp.bfloat16
CHUNK_OWNERS = (0, 2, 1, 3)


def dot(left, right):
    return jnp.dot(left, right, preferred_element_type=F32)


def dot_rows(left, right):
    return lax.dot_general(left, right, (((0,), (0,)), ((), ())), preferred_element_type=F32)


def dot_columns(left, right):
    return lax.dot_general(left, right, (((1,), (1,)), ((), ())), preferred_element_type=F32)


def gather_ctx(part):
    copies = jnp.broadcast_to(part[None], (lax.axis_size("ctx"), *part.shape))
    return lax.all_to_all(copies, "ctx", 0, 0, tiled=True)


def sum_ctx(parts):
    return jnp.sum(lax.all_to_all(parts, "ctx", 0, 0, tiled=True).astype(F32), axis=0)


def after(value, *others):
    for other in others:
        first = lax.slice(other, (0,) * other.ndim, (1,) * other.ndim).reshape(())
        value = value + (first * 0).astype(value.dtype)
    return value


LINKS = ((1, 1), (2, 1), (0, 1), (2, 3), (0, 3))
GRID = (4, 2, 4)


def grid_place(index):
    return (index // 8, index // 4 % 2, index % 4)


def across_link(value, link):
    axis, distance = link

    def partner(device):
        place = list(grid_place(device))
        place[axis] ^= distance
        return (place[0] * GRID[1] + place[1]) * GRID[2] + place[2]

    size = lax.axis_size("ctx")
    return lax.ppermute(value, "ctx", [(i, partner(i)) for i in range(size)])


def cut(value, axis, start, stop):
    return lax.slice_in_dim(value, start, stop, axis=axis)


def join_halves(mine, theirs, link, place):
    axis, distance = link
    both = [mine, theirs]
    if GRID[axis] == 2 or (distance == 1 and mine.shape[axis] == 1):
        second = place[axis] % 2 == 1
    elif distance == 3:
        second = place[axis] >= 2
    else:
        outer = (place[axis] == 0) | (place[axis] == 3)
        ends, middle = jnp.where(outer, mine, theirs), jnp.where(outer, theirs, mine)
        return jnp.concatenate([cut(ends, axis, 0, 1), middle, cut(ends, axis, 1, 2)], axis=axis)
    return jnp.where(
        second,
        jnp.concatenate(both[::-1], axis=axis),
        jnp.concatenate(both, axis=axis),
    )


def link_of(step, part):
    return LINKS[(step + part) % len(LINKS)]


def link_mask(link):
    axis, distance = link
    return distance * (8, 4, 1)[axis]


def place_masks(part):
    masks = [0]
    for step in range(len(LINKS)):
        masks = masks + [mask ^ link_mask(link_of(step, part)) for mask in masks]
    return masks


def gather_step(parts, step):
    return [
        jnp.concatenate([part, across_link(part, link_of(step, at))])
        for at, part in enumerate(parts)
    ]


def gather_in_place(part, at):
    place = grid_place(lax.axis_index("ctx"))
    part = part[None, None, None]
    for step in range(len(LINKS)):
        link = link_of(step, at)
        part = join_halves(part, across_link(part, link), link, place)
    return part.reshape(-1, part.shape[-1])


def sum_links(pairs):
    for step in reversed(range(len(LINKS))):
        sums = [
            kept.astype(F32) + across_link(sent, link_of(step, at)).astype(F32)
            for at, (kept, sent) in enumerate(pairs)
        ]
        pairs = []
        for total in sums:
            half = total.shape[0] // 2
            total = total.astype(BF16) if step else total
            pairs.append((total[:half], total[half:]))
    return [total[0] for total in sums]


def across_ep(value, distance):
    return lax.ppermute(value, "ep", [(i, i ^ distance) for i in range(4)])


def gather_ep(rows, axis):
    half = jnp.concatenate([rows, across_ep(rows, 2)], axis=axis)
    return jnp.concatenate([half, across_ep(half, 1)], axis=axis)


def finish_sum(kept, received):
    half = kept + received.astype(F32)
    size = half.shape[1] // 2
    return half[:, :size] + across_ep(half[:, size:].astype(BF16), 2).astype(F32)


def sum_ep(rows, axis, sent_as=BF16):
    size = rows.shape[axis] // 4

    kept, sent = cut(rows, axis, 0, 2 * size), cut(rows, axis, 2 * size, 4 * size)
    half = kept.astype(F32) + across_ep(sent.astype(sent_as), 1).astype(F32)
    kept, sent = cut(half, axis, 0, size), cut(half, axis, size, 2 * size)
    return kept + across_ep(sent.astype(sent_as), 2).astype(F32)


def quad_member(device, size, distance):
    planes, plane = 4, size // 4
    slot, place = device // plane, device % plane
    if distance % 2:
        place = plane - 1 - place
    return (slot ^ distance) % planes * plane + place


def quad_block(ctx, size, distance):
    plane = size // 4
    slot, place = ctx // plane, ctx % plane
    if distance % 2:
        place = plane - 1 - place
    return (slot ^ distance) * plane + place


def across_quad(value, distance):
    size = lax.axis_size("ctx")
    return lax.ppermute(
        value, "ctx", [(i, quad_member(i, size, distance)) for i in range(size)]
    )


def swap_quad(parts):
    return [parts[0]] + [across_quad(parts[distance], distance) for distance in range(1, 4)]


def pick(parts, index):
    return lax.dynamic_index_in_dim(parts, index, 0, keepdims=False)


def rms_scale(values):
    return lax.rsqrt(jnp.mean(values * values, axis=-1, keepdims=True) + EPSILON)


def rope_tables(positions):
    inverse = jnp.exp(
        jnp.arange(HALF, dtype=F32) * (-2.0 * math.log(10000.0) / HEAD_DIM)
    )
    angles = inverse[:, None] * positions.astype(F32)[..., None, :]
    return jnp.cos(angles), jnp.sin(angles)


def rotate(values, cosine, sine):
    first, second = values[..., :HALF, :], values[..., HALF:, :]
    return jnp.concatenate(
        [first * cosine - second * sine, second * cosine + first * sine], axis=-2
    )


def unrotate(values, cosine, sine):
    first, second = values[..., :HALF, :], values[..., HALF:, :]
    return jnp.concatenate(
        [first * cosine + second * sine, second * cosine - first * sine], axis=-2
    )


def widen(heads_ref, side, target_ref, offset):
    target_ref[...] = jnp.zeros_like(target_ref)
    for head in range(GROUP):
        target_ref[offset : offset + HEAD_DIM, head * BLOCK : (head + 1) * BLOCK] = heads_ref[
            side, head
        ]


def allowed_pairs(key_block, query_block, key_segments, query_segments, row_ref, col_ref):
    keys = col_ref[:, 0:1] + key_block * BLOCK
    queries = row_ref[...] + query_block * BLOCK
    return (key_segments == query_segments) & (keys <= queries)


def forward_kernel(
    blocks_ref,
    q_ref,
    kv_ref,
    seg_row_ref,
    seg_col_ref,
    row_ref,
    col_ref,
    o_ref,
    lse_ref,
    q_wide,
    top,
    total,
    acc,
):
    def one_side(side, nothing):
        query_block = blocks_ref[side]
        widen(q_ref, side, q_wide, 0)
        top[...] = jnp.full_like(top, MASKED)
        total[...] = jnp.zeros_like(total)
        acc[...] = jnp.zeros_like(acc)
        query_segments = seg_row_ref[side]
        covered = query_segments == COVERING

        def add(block, scores, scale_by, new_top):
            weights = jnp.exp(scores - scale_by)
            shrink = jnp.exp(top[...] - new_top)
            top[...] = new_top
            total[...] = total[...] * shrink + jnp.sum(weights, axis=0, keepdims=True)
            added = dot_rows(kv_ref[block], weights.astype(BF16))[HEAD_DIM:]
            acc[...] = acc[...] * shrink + added

        def edge(block, column):
            scores = dot(kv_ref[block], q_wide[...])
            allowed = allowed_pairs(
                block, query_block, seg_col_ref[column][:, 0:1], query_segments, row_ref, col_ref
            )
            scores = jnp.where(allowed, scores, MASKED)
            new_top = jnp.maximum(top[...], jnp.max(scores, axis=0, keepdims=True))
            add(block, scores, new_top, new_top)

        def inner(block, carry):
            scores = dot(kv_ref[block], q_wide[...])
            new_top = jnp.maximum(top[...], jnp.max(scores, axis=0, keepdims=True))
            add(
                block,
                scores,
                jnp.where(covered, new_top, -MASKED),
                jnp.where(covered, new_top, top[...]),
            )
            return carry

        @pl.when(query_block > 0)
        def _():
            edge(0, COMBOS)

        lax.fori_loop(1, query_block, inner, 0)
        edge(query_block, side)
        lse_ref[side] = top[...] + jnp.log(total[...])
        result = acc[...] / total[...]
        for head in range(GROUP):
            o_ref[side, head] = result[:, head * BLOCK : (head + 1) * BLOCK]
        return nothing

    lax.fori_loop(0, COMBOS, one_side, 0)


def backward_kernel(
    blocks_ref,
    q_ref,
    do_ref,
    kv_ref,
    o_ref,
    lse_ref,
    seg_row_ref,
    seg_col_ref,
    row_ref,
    col_ref,
    cos_ref,
    sin_ref,
    dq_ref,
    dkv_ref,
    q_wide,
    do_wide,
    q_tall,
    do_tall,
    dq_acc,
    dkv_acc,
):
    dkv_acc[...] = jnp.zeros_like(dkv_acc)

    def one_side(side, nothing):
        query_block = blocks_ref[side]
        widen(q_ref, side, q_wide, 0)
        widen(do_ref, side, do_wide, HEAD_DIM)
        for head in range(GROUP):
            at = slice(head * BLOCK, (head + 1) * BLOCK)
            q_tall[at, :] = q_wide[:, at].astype(F32).T.astype(BF16)
            do_tall[at, :] = do_wide[:, at].astype(F32).T.astype(BF16)
        dq_acc[...] = jnp.zeros_like(dq_acc)
        query_segments = seg_row_ref[side]
        lse = lse_ref[side]
        covered_lse = jnp.where(query_segments == COVERING, lse, -MASKED)
        delta = jnp.concatenate(
            [
                jnp.sum(
                    o_ref[side, head] * do_ref[side, head].astype(F32), axis=0, keepdims=True
                )
                for head in range(GROUP)
            ],
            axis=1,
        )

        def add(block, scores, scale_by):
            weights = jnp.exp(scores - scale_by)
            grad_weights = dot(kv_ref[block], do_wide[...])
            grad_scores = (weights * (grad_weights - delta)).astype(BF16)
            dkv_acc[block] += dot(grad_scores, q_tall[...]) + dot(
                weights.astype(BF16), do_tall[...]
            )
            dq_acc[...] += dot_rows(kv_ref[block], grad_scores)[:HEAD_DIM]

        def edge(block, column):
            scores = dot(kv_ref[block], q_wide[...])
            allowed = allowed_pairs(
                block, query_block, seg_col_ref[column][:, 0:1], query_segments, row_ref, col_ref
            )
            add(block, jnp.where(allowed, scores, MASKED), lse)

        def inner(block, carry):
            add(block, dot(kv_ref[block], q_wide[...]), covered_lse)
            return carry

        @pl.when(query_block > 0)
        def _():
            edge(0, COMBOS)

        lax.fori_loop(1, query_block, inner, 0)
        edge(query_block, side)
        for head in range(GROUP):
            at = slice(head * BLOCK, (head + 1) * BLOCK)
            grad = unrotate(dq_acc[:, at], cos_ref[side], sin_ref[side])
            dq_ref[side, head] = (grad * (1.0 / math.sqrt(HEAD_DIM))).astype(BF16)
        return nothing

    lax.fori_loop(0, COMBOS, one_side, 0)
    dkv_ref[...] = dkv_acc[...].astype(BF16)


def experts_kernel(
    places_ref,
    ep_ref,
    tokens_ref,
    cotangent_ref,
    gates_ref,
    *refs,
):
    halves, refs = refs[:8], refs[8:]
    grad_kept, grad_sent, out_kept, out_sent, pre_ref, hidden_ref = refs[:6]
    weights, grad_acc, out_acc, gate_acc, arrived = refs[6:]
    quarter = hidden_ref.shape[2]
    rows = tokens_ref.shape[0]
    block_rows = halves[0].shape[1]
    width = tokens_ref.shape[1]

    def fetch(q):
        for half in range(2):
            source = halves[2 * q + half]
            for at in range(source.shape[0]):
                start = places_ref[q, half * source.shape[0] + at] * block_rows
                start = pl.multiple_of(start, 16)
                pltpu.make_async_copy(
                    source.at[at],
                    weights.at[q % 2, pl.ds(start, block_rows)],
                    arrived.at[q % 2],
                ).start()

    fetch(0)
    gate_acc[...] = jnp.zeros_like(gate_acc)
    for q in range(4):
        if q < 3:
            fetch(q + 1)
        pltpu.make_async_copy(weights.at[q % 2], weights.at[q % 2], arrived.at[q % 2]).wait()
        weights_in = weights[q % 2, :, : 2 * quarter]
        weights_out = weights[q % 2, :, 2 * quarter :]
        grad_hidden = dot(cotangent_ref[...], weights_out)
        pre = dot(tokens_ref[...], weights_in)
        gate_pre, up_pre = pre[:, :quarter], pre[:, quarter:]
        sigmoid = 1.0 / (1.0 + jnp.exp(-gate_pre))
        activated = gate_pre * sigmoid
        hidden = activated * up_pre
        products = grad_hidden * hidden
        tiles = [(tile, (q * quarter // 128 + tile) // 4) for tile in range(quarter // 128)]
        gates = jnp.concatenate(
            [
                jnp.broadcast_to(gates_ref[:, expert : expert + 1], (rows, 128))
                for _, expert in tiles
            ],
            axis=1,
        )
        for tile, expert in tiles:
            gate_acc[expert] += products[:, tile * 128 : (tile + 1) * 128]
        gated_hidden = (gates * hidden).astype(BF16)
        grad_hidden = gates * grad_hidden
        pre_ref[q, :, :quarter] = (
            grad_hidden * up_pre * sigmoid * (1.0 + gate_pre * (1.0 - sigmoid))
        ).astype(BF16)
        pre_ref[q, :, quarter:] = (grad_hidden * activated).astype(BF16)
        hidden_ref[q] = gated_hidden
        grad = dot_columns(pre_ref[q], weights_in)
        out = dot_columns(gated_hidden, weights_out)
        if q == 0:
            grad_acc[...] = grad
            out_acc[...] = out
        elif q < 3:
            grad_acc[...] += grad
            out_acc[...] += out
        else:
            for batch in range(MB):
                kept = slice(batch * BLOCK, batch * BLOCK + BLOCK // 2)
                sent = slice(batch * BLOCK + BLOCK // 2, (batch + 1) * BLOCK)
                grad_kept[batch, :, :width] = grad_acc[kept] + grad[kept]
                grad_sent[batch, :, :width] = (grad_acc[sent] + grad[sent]).astype(BF16)
                out_kept[batch] = out_acc[kept] + out[kept]
                out_sent[batch] = (out_acc[sent] + out[sent]).astype(BF16)
    columns = lax.broadcasted_iota(jnp.int32, (rows, 128), 1) - ep_ref[0] * EXP_DEV
    message = jnp.zeros((rows, 128), F32)
    for expert in range(EXP_DEV):
        total = jnp.sum(gate_acc[expert], axis=1, keepdims=True)
        high = total.astype(BF16).astype(F32)
        message = jnp.where(columns == expert, high, message)
        message = jnp.where(columns == expert + EXPERTS, total - high, message)
    for batch in range(MB):
        start = batch * BLOCK
        grad_kept[batch, :, width:] = message[start : start + BLOCK // 2]
        grad_sent[batch, :, width:] = message[start + BLOCK // 2 : start + BLOCK].astype(BF16)


def expert_grads_kernel(
    places_ref, tokens_ref, cotangent_ref, pre_ref, hidden_ref, kept_ref, sent_ref, scratch
):
    half, block_rows, _ = kept_ref.shape
    planes, quarter = 4, hidden_ref.shape[2]
    rows = tokens_ref.shape[1] // planes
    blocks = rows // block_rows
    for plane in range(planes):
        at = slice(plane * rows, (plane + 1) * rows)
        scratch[:, : 2 * quarter] = dot_rows(tokens_ref[:, at], pre_ref[0]).astype(BF16)
        scratch[:, 2 * quarter :] = dot_rows(cotangent_ref[:, at], hidden_ref[0]).astype(BF16)
        for block in range(blocks):
            place = places_ref[plane * blocks + block]
            value = scratch[block * block_rows : (block + 1) * block_rows, :]

            @pl.when(place < half)
            def _():
                kept_ref[place] = value

            @pl.when(place >= half)
            def _():
                sent_ref[place - half] = value


SMEM_SPEC = pl.BlockSpec(memory_space=pltpu.SMEM)
VMEM_SPEC = pl.BlockSpec(memory_space=pltpu.VMEM)
HEADS_SHAPE = (COMBOS, GROUP, HEAD_DIM, BLOCK)


ANY_SPEC = pl.BlockSpec(memory_space=pl.ANY)


def run_experts(places, ep, tokens, cotangent, gates, halves):
    rows, width = tokens.shape
    _, block_rows, columns = halves[0].shape
    quarter = columns // 3
    kept_rows = (MB, BLOCK // 2)
    return pl.pallas_call(
        experts_kernel,
        out_shape=(
            jax.ShapeDtypeStruct((*kept_rows, width + 128), F32),
            jax.ShapeDtypeStruct((*kept_rows, width + 128), BF16),
            jax.ShapeDtypeStruct((*kept_rows, width), F32),
            jax.ShapeDtypeStruct((*kept_rows, width), BF16),
            jax.ShapeDtypeStruct((4, rows, 2 * quarter), BF16),
            jax.ShapeDtypeStruct((4, rows, quarter), BF16),
        ),
        in_specs=[SMEM_SPEC] * 2 + [VMEM_SPEC] * 3 + [ANY_SPEC] * 8,
        out_specs=(VMEM_SPEC,) * 6,
        scratch_shapes=[
            pltpu.VMEM((2, width, columns), BF16),
            pltpu.VMEM((rows, width), F32),
            pltpu.VMEM((rows, width), F32),
            pltpu.VMEM((EXP_DEV, rows, 128), F32),
            pltpu.SemaphoreType.DMA((2,)),
        ],
        compiler_params=pltpu.CompilerParams(vmem_limit_bytes=50 * 1024 * 1024),
        cost_estimate=pl.CostEstimate(
            flops=16 * rows * width * columns,
            bytes_accessed=30 * 1024 * 1024,
            transcendentals=4 * rows * quarter,
        ),
        name="run_experts",
    )(places, ep, tokens, cotangent, gates, *halves)


def expert_grads(q, places, tokens, cotangent, pre, hidden, block_rows):
    rows, width = tokens.shape
    quarter = hidden.shape[2]
    half = jax.ShapeDtypeStruct((width // block_rows // 2, block_rows, 3 * quarter), BF16)
    whole = pl.BlockSpec((rows, width), lambda i: (0, 0))
    return pl.pallas_call(
        expert_grads_kernel,
        grid=(1,),
        out_shape=(half, half),
        in_specs=[
            SMEM_SPEC,
            whole,
            whole,
            pl.BlockSpec((1, rows, 2 * quarter), lambda i: (q, 0, 0)),
            pl.BlockSpec((1, rows, quarter), lambda i: (q, 0, 0)),
        ],
        out_specs=(pl.BlockSpec(half.shape, lambda i: (0, 0, 0)),) * 2,
        scratch_shapes=[pltpu.VMEM((width // 4, 3 * quarter), BF16)],
        compiler_params=pltpu.CompilerParams(vmem_limit_bytes=40 * 1024 * 1024),
        cost_estimate=pl.CostEstimate(
            flops=6 * rows * width * quarter,
            bytes_accessed=8 * 1024 * 1024,
            transcendentals=0,
        ),
        name="expert_grads",
    )(places, tokens, cotangent, pre, hidden)


def attend(blocks, queries, keys_values, *places):
    steps = 2 * keys_values.shape[0] + 2
    return pl.pallas_call(
        forward_kernel,
        out_shape=(
            jax.ShapeDtypeStruct(HEADS_SHAPE, F32),
            jax.ShapeDtypeStruct((COMBOS, 1, LANES), F32),
        ),
        in_specs=[SMEM_SPEC] + [VMEM_SPEC] * 6,
        out_specs=(VMEM_SPEC, VMEM_SPEC),
        scratch_shapes=[
            pltpu.VMEM((2 * HEAD_DIM, LANES), BF16),
            pltpu.VMEM((1, LANES), F32),
            pltpu.VMEM((1, LANES), F32),
            pltpu.VMEM((HEAD_DIM, LANES), F32),
        ],
        compiler_params=pltpu.CompilerParams(vmem_limit_bytes=32 * 1024 * 1024),
        cost_estimate=pl.CostEstimate(
            flops=steps * 8 * BLOCK * LANES * HEAD_DIM,
            bytes_accessed=4 * 1024 * 1024,
            transcendentals=steps * BLOCK * LANES,
        ),
        name="attend",
    )(blocks, queries, keys_values, *places)


def attend_back(blocks, queries, grads, keys_values, mixed, lse, *places):
    steps = 2 * keys_values.shape[0] + 2
    return pl.pallas_call(
        backward_kernel,
        out_shape=(
            jax.ShapeDtypeStruct(HEADS_SHAPE, BF16),
            jax.ShapeDtypeStruct(keys_values.shape, BF16),
        ),
        in_specs=[SMEM_SPEC] + [VMEM_SPEC] * 11,
        out_specs=(VMEM_SPEC, VMEM_SPEC),
        scratch_shapes=[
            pltpu.VMEM((2 * HEAD_DIM, LANES), BF16),
            pltpu.VMEM((2 * HEAD_DIM, LANES), BF16),
            pltpu.VMEM((LANES, 2 * HEAD_DIM), BF16),
            pltpu.VMEM((LANES, 2 * HEAD_DIM), BF16),
            pltpu.VMEM((HEAD_DIM, LANES), F32),
            pltpu.VMEM(keys_values.shape, F32),
        ],
        compiler_params=pltpu.CompilerParams(vmem_limit_bytes=40 * 1024 * 1024),
        cost_estimate=pl.CostEstimate(
            flops=steps * 20 * BLOCK * LANES * HEAD_DIM,
            bytes_accessed=6 * 1024 * 1024,
            transcendentals=steps * BLOCK * LANES,
        ),
        name="attend_back",
    )(blocks, queries, grads, keys_values, mixed, lse, *places)


def local(
    inputs,
    cotangent,
    segments,
    routes,
    attn_gain,
    w_query,
    key_weight,
    value_weight,
    w_out,
    ffn_gain,
    router,
    w_gate,
    w_up,
    w_down,
):
    ctx_count = lax.axis_size("ctx")
    ctx = lax.axis_index("ctx")
    ep = lax.axis_index("ep")
    slot = ctx // (ctx_count // 4)
    blocks = jnp.stack([quad_block(ctx, ctx_count, distance) for distance in range(4)])
    rows_weight = w_query.shape[0]
    token_rows = inputs.shape[1]
    width = inputs.shape[2]
    hidden_width = w_gate.shape[2]
    width_query = w_query.shape[1]
    width_key = key_weight.shape[1]
    width_joined = width_query + 2 * width_key
    side_start = width_joined
    small_rows = attn_gain.shape[0]
    owners = [ep ^ owner for owner in CHUNK_OWNERS]

    in_width = EXP_DEV * hidden_width
    quarter = in_width // 4
    expert_rows = [
        jnp.concatenate([w_gate[e] for e in range(EXP_DEV)], axis=1),
        jnp.concatenate([w_up[e] for e in range(EXP_DEV)], axis=1),
        jnp.concatenate([w_down[e].T for e in range(EXP_DEV)], axis=1),
    ]
    weight_parts = [
        jnp.concatenate([rows[:, q * quarter : (q + 1) * quarter] for rows in expert_rows], axis=1)
        for q in range(4)
    ]
    expert_ids = jnp.arange(EXPERTS, dtype=jnp.int32)
    chosen_own = jnp.any(routes[..., None] == expert_ids, axis=2).astype(BF16)
    small_own = jnp.concatenate([attn_gain[:, None], ffn_gain[:, None], router], axis=1)
    small_width = small_own.shape[1]
    small_parts = gather_ep(
        jnp.pad(small_own, ((0, 16 - small_rows), (0, 128 - small_width)))[None], 0
    )[:, :small_rows, :small_width]
    natural = [pick(jnp.asarray(CHUNK_OWNERS), ep ^ part) for part in range(4)]
    small_group = jnp.concatenate([pick(small_parts, part) for part in natural])
    chosen = (
        gather_ep(jnp.pad(chosen_own, ((0, 0), (0, 0), (0, 128 - EXPERTS))), 1)[..., :EXPERTS]
        .reshape(MB * BLOCK, EXPERTS)
    ) > 0
    segment_parts = segments.reshape(MB, 4, token_rows).transpose(1, 0, 2)
    segments_here = jnp.stack([pick(segment_parts, owner) for owner in owners], axis=1)
    seg_width = -(-MB * BLOCK // rows_weight)
    seg_part = jnp.pad(
        segments_here.reshape(-1).astype(BF16), (0, seg_width * rows_weight - MB * BLOCK)
    ).reshape(rows_weight, seg_width)
    side_part = jnp.concatenate([small_group, seg_part], axis=1)
    joined_part = jnp.concatenate(
        [
            w_query,
            key_weight,
            value_weight,
            jnp.pad(side_part, ((0, 0), (0, 128 - side_part.shape[1]))),
        ],
        axis=1,
    )
    inputs_all = gather_ep(inputs, 1).reshape(MB * BLOCK, width)
    joined_all = gather_ctx(after(joined_part, inputs_all))
    joined = joined_all[:, :, :width_joined].reshape(width, width_joined)
    side_all = joined_all[:, :, side_start:].reshape(width, 128)
    experts = [after(part, joined_all)[None] for part in weight_parts]
    w_out_all = gather_in_place(after(w_out.T, joined_all), 4)
    for step in range(4):
        experts = gather_step(experts, step)
    expert_halves = [
        half
        for at, part in enumerate(experts)
        for half in (part, across_link(part, link_of(4, at)))
    ]
    masks = jnp.asarray([place_masks(part) for part in range(4)], jnp.int32)
    expert_places = masks ^ ctx
    grad_places = jnp.stack(
        [
            jnp.asarray([place_masks(part).index(mask) for mask in range(ctx_count)], jnp.int32)[
                jnp.arange(ctx_count, dtype=jnp.int32) ^ ctx
            ]
            for part in range(4)
        ]
    )
    gain_one = side_all[:, 0].astype(F32)
    gain_two = side_all[:, 1].astype(F32)
    router_full = side_all[:, 2 : 2 + EXPERTS]
    seg_all = (
        joined_all[:, :, side_start + small_width : side_start + side_part.shape[1]]
        .reshape(ctx_count, -1)[:, : MB * BLOCK]
        .reshape(ctx_count, MB, BLOCK)
        .astype(F32)
    )
    cotangent_all = gather_ep(cotangent, 1).reshape(MB * BLOCK, width)

    offsets = (
        jnp.stack(owners)[:, None] * token_rows + jnp.arange(token_rows, dtype=jnp.int32)
    ).reshape(BLOCK)
    cosines, sines = rope_tables(blocks[:, None] * BLOCK + offsets)
    cosine_both, sine_both = jnp.tile(cosines[0], (1, MB)), jnp.tile(sines[0], (1, MB))

    def by_combo(heads):
        rows = heads.shape[0] // KV_DEV
        parts = heads.reshape(KV_DEV, rows, MB, BLOCK).transpose(2, 0, 1, 3)
        return parts.reshape(COMBOS, rows, BLOCK)

    def from_combos(parts):
        rows = parts.shape[1]
        parts = parts.reshape(MB, KV_DEV, rows, BLOCK).transpose(1, 2, 0, 3)
        return parts.reshape(KV_DEV * rows, MB * BLOCK)

    def to_attention(heads):
        parts = by_combo(heads).reshape(HEADS_SHAPE)
        return jnp.stack(swap_quad([pick(parts, slot ^ distance) for distance in range(4)]))

    def from_attention(parts):
        parts = jnp.stack(swap_quad([parts[distance] for distance in range(4)]))
        parts = jnp.stack([pick(parts, slot ^ combo) for combo in range(COMBOS)])
        return from_combos(parts.reshape(COMBOS, GROUP * HEAD_DIM, BLOCK))

    values = inputs_all.astype(F32)
    scale_one = rms_scale(values)
    normal_one = values * scale_one
    normed = (normal_one * gain_one).astype(BF16)
    projected = jnp.einsum("td,dc->ct", normed, joined, preferred_element_type=F32)

    def turned(start, stop):
        heads = projected[start:stop].reshape(-1, HEAD_DIM, MB * BLOCK)
        return rotate(heads, cosine_both, sine_both).astype(BF16).reshape(-1, MB * BLOCK)

    keys = by_combo(turned(width_query, width_query + width_key))
    key_values = jnp.concatenate(
        [keys, by_combo(projected[width_query + width_key :].astype(BF16))], axis=1
    ).transpose(0, 2, 1)
    sent = jnp.broadcast_to(
        key_values[:, None], (COMBOS, ctx_count // COMBOS, BLOCK, 2 * HEAD_DIM)
    ).reshape(ctx_count, BLOCK, 2 * HEAD_DIM)
    keys_values = lax.all_to_all(sent, "ctx", 0, 0, tiled=True)
    queries = to_attention(turned(0, width_query) * jnp.asarray(1.0 / math.sqrt(HEAD_DIM), BF16))
    seg_here = pick(seg_all.transpose(1, 0, 2), slot // KV_DEV)
    seg_sides = jnp.stack([pick(seg_here, blocks[side]) for side in range(COMBOS)])
    seg_rows = jnp.tile(seg_sides, (1, GROUP))[:, None, :]
    seg_columns = jnp.broadcast_to(
        jnp.concatenate([seg_sides, seg_here[:1]])[:, :, None], (COMBOS + 1, BLOCK, 128)
    )
    offset_row = jnp.tile(offsets, GROUP)[None, :]
    offset_column = jnp.broadcast_to(offsets[:, None], (BLOCK, 128))
    places = (seg_rows, seg_columns, offset_row, offset_column)
    mixed_parts, lse = attend(
        after(blocks, cotangent_all, chosen.astype(F32), *experts), queries, keys_values, *places
    )
    mixed = from_attention(mixed_parts.astype(BF16))

    attn = jnp.einsum("ht,dh->td", mixed, w_out_all, preferred_element_type=F32)
    attn = sum_ep(attn.reshape(MB, BLOCK, width), 1)
    residual = inputs.astype(F32) + attn
    scale_two = rms_scale(residual)
    normal_two = residual * scale_two
    tokens = (normal_two * gain_two).astype(BF16)
    tokens_all = gather_ep(tokens, 1).reshape(MB * BLOCK, width)

    logits = dot(tokens_all, router_full)
    gates = jax.nn.softmax(jnp.where(chosen, logits, MASKED), axis=-1)
    gates_own = gates.reshape(MB, BLOCK, EXPERTS)[:, :token_rows]
    gates_here = lax.dynamic_slice_in_dim(gates, ep * EXP_DEV, EXP_DEV, axis=1)
    grad_kept, grad_sent, out_kept, out_sent, grad_pre, gated_hidden = run_experts(
        expert_places,
        ep.astype(jnp.int32)[None],
        tokens_all,
        cotangent_all,
        jnp.pad(gates_here, ((0, 0), (0, 128 - EXP_DEV))),
        expert_halves,
    )
    received = across_ep(grad_sent, 1)
    message = finish_sum(grad_kept, received)
    grad_places = after(grad_places, received)
    grad_parts = sum_links(
        [
            expert_grads(
                q, grad_places[q], tokens_all, cotangent_all, grad_pre, gated_hidden, rows_weight
            )
            for q in range(4)
        ]
    )
    outputs = (residual + finish_sum(out_kept, across_ep(out_sent, 1))).astype(BF16)

    grad_gates = (
        message[..., width : width + EXPERTS]
        + message[..., width + EXPERTS : width + 2 * EXPERTS]
    )
    grad_logits = (
        gates_own * (grad_gates - jnp.sum(gates_own * grad_gates, axis=-1, keepdims=True))
    ).astype(BF16)
    grad_tokens = message[..., :width] + jnp.einsum(
        "bte,de->btd", grad_logits, router_full, preferred_element_type=F32
    )
    grad_router = jnp.einsum("btd,bte->de", tokens, grad_logits, preferred_element_type=F32)
    grad_gain_two = jnp.sum(grad_tokens * normal_two, axis=(0, 1))
    scaled = grad_tokens * gain_two
    grad_residual = cotangent.astype(F32) + scale_two * (
        scaled - normal_two * jnp.mean(scaled * normal_two, axis=-1, keepdims=True)
    )
    grad_attn = gather_ep(grad_residual.astype(BF16), 1).reshape(MB * BLOCK, width)
    grad_mixed = jnp.einsum(
        "td,dh->ht", grad_attn, w_out_all, preferred_element_type=F32
    ).astype(BF16)
    grad_mixed = to_attention(grad_mixed)

    small_grads = jnp.concatenate([grad_gain_two[:, None], grad_router], axis=1)
    small_high = lax.reduce_precision(small_grads, 8, 7)
    small_count = small_grads.shape[1]
    grad_out = jnp.einsum("td,ht->dh", grad_attn, mixed, preferred_element_type=F32)
    grad_out = jnp.concatenate(
        [
            grad_out.astype(BF16),
            small_high.astype(BF16),
            (small_grads - small_high).astype(BF16),
            jnp.zeros((width, 128 - 2 * small_count), BF16),
        ],
        axis=1,
    )
    blocks = after(blocks, grad_out, outputs)
    grad_out = sum_ctx(grad_out.reshape(ctx_count, rows_weight, width_query + 128))
    small_grads = (
        grad_out[:, width_query : width_query + small_count]
        + grad_out[:, width_query + small_count : width_query + 2 * small_count]
    )
    grad_out = grad_out[:, :width_query].T

    grad_queries, grad_keys_values = attend_back(
        blocks,
        queries,
        grad_mixed,
        keys_values,
        mixed_parts,
        lse,
        *places,
        cosines,
        sines,
    )
    received = lax.all_to_all(grad_keys_values, "ctx", 0, 0, tiled=True).astype(F32)
    received = jnp.sum(
        received.reshape(COMBOS, ctx_count // COMBOS, BLOCK, 2 * HEAD_DIM), axis=1
    ).transpose(0, 2, 1)
    grad_query = from_attention(grad_queries)
    grad_key = unrotate(received[:, :HEAD_DIM], cosines[0], sines[0])
    grad_kv = jnp.concatenate(
        [
            from_combos(grad_key.astype(BF16)),
            from_combos(received[:, HEAD_DIM:].astype(BF16)),
        ]
    )
    grad_partial = dot_rows(
        jnp.concatenate([grad_query, grad_kv]), joined.T
    )
    grad_normed = sum_ep(grad_partial.reshape(MB, BLOCK, width), 1)
    values = inputs.astype(F32)
    scale_own = rms_scale(values)
    normal_own = values * scale_own
    scaled = grad_normed * gain_one
    input_grads = (
        grad_residual
        + scale_own
        * (scaled - normal_own * jnp.mean(scaled * normal_own, axis=-1, keepdims=True))
    ).astype(BF16)

    grad_joined = jnp.concatenate([grad_query, grad_kv])
    grad_joined = jnp.einsum("td,ct->dc", normed, grad_joined, preferred_element_type=F32)
    grad_joined = sum_ctx(
        grad_joined.astype(BF16).reshape(ctx_count, rows_weight, width_joined)
    )
    grad_w_query = grad_joined[:, :width_query]
    grad_w_kv = grad_joined[:, width_query:]
    grad_gain_one = jnp.sum(
        grad_joined * joined_part[:, :width_joined].astype(F32), axis=1, keepdims=True
    ) / side_part[:, :1].astype(F32)
    small_grads = jnp.concatenate([grad_gain_one, small_grads], axis=1)
    small_grads = jnp.pad(small_grads, ((0, 0), (0, 128 - 1 - small_count)))
    small_grads = small_grads.reshape(4, small_rows, 128)
    small_grads = jnp.stack([pick(small_grads, owner) for owner in owners])
    small_grads = sum_ep(small_grads, 0, F32)[0, :, : 1 + small_count]
    def by_expert(which):
        at = slice(which * quarter, (which + 1) * quarter)
        grad = jnp.concatenate([part[:, at] for part in grad_parts], axis=1)
        return jnp.stack(
            [grad[:, e * hidden_width : (e + 1) * hidden_width] for e in range(EXP_DEV)]
        )

    return (
        outputs,
        input_grads,
        small_grads[:, 0],
        grad_w_query,
        grad_w_kv[:, :width_key],
        grad_w_kv[:, width_key:],
        grad_out,
        small_grads[:, 1],
        small_grads[:, 2:],
        by_expert(0),
        by_expert(1),
        by_expert(2).transpose(0, 2, 1),
    )


def solution(mesh):
    rows = P(None, ("ctx", "ep"), None)
    shared = P(("ctx", "ep"))
    weight = P("ctx", "ep")
    out_weight = P("ep", "ctx")
    expert = P("ep", "ctx", None)
    down = P("ep", None, "ctx")
    router = P(("ctx", "ep"), None)
    return jax.shard_map(
        local,
        mesh=mesh,
        in_specs=(
            rows,
            rows,
            P(None, "ctx"),
            rows,
            shared,
            weight,
            weight,
            weight,
            out_weight,
            shared,
            router,
            expert,
            expert,
            down,
        ),
        out_specs=(
            rows,
            rows,
            shared,
            weight,
            weight,
            weight,
            out_weight,
            shared,
            router,
            expert,
            expert,
            down,
        ),
        check_vma=False,
    )
```

```python
import math

import jax
import jax.numpy as jnp
from jax import lax
from jax.experimental import pallas as pl
from jax.experimental.pallas import tpu as pltpu
from jax.sharding import PartitionSpec as P

HEAD_DIM = 64
HALF = 32
GROUP = 3
KV_DEV = 2
EXP_DEV = 3
EXPERTS = 12
MB = 2
COMBOS = MB * KV_DEV
BLOCK = 256
LANES = GROUP * BLOCK
COVERING = 4.0
EPSILON = 1e-06
MASKED = -1e30
F32 = jnp.float32
BF16 = jnp.bfloat16
CHUNK_OWNERS = (0, 2, 1, 3)


def dot(left, right):
    return jnp.dot(left, right, preferred_element_type=F32)


def dot_rows(left, right):
    return lax.dot_general(left, right, (((0,), (0,)), ((), ())), preferred_element_type=F32)


def dot_columns(left, right):
    return lax.dot_general(left, right, (((1,), (1,)), ((), ())), preferred_element_type=F32)


def gather_ctx(part):
    copies = jnp.broadcast_to(part[None], (lax.axis_size("ctx"), *part.shape))
    return lax.all_to_all(copies, "ctx", 0, 0, tiled=True)


def sum_ctx(parts):
    return jnp.sum(lax.all_to_all(parts, "ctx", 0, 0, tiled=True).astype(F32), axis=0)


def after(value, *others):
    for other in others:
        first = lax.slice(other, (0,) * other.ndim, (1,) * other.ndim).reshape(())
        value = value + (first * 0).astype(value.dtype)
    return value


LINKS = ((1, 1), (2, 1), (0, 1), (2, 3), (0, 3))
GRID = (4, 2, 4)


def grid_place(index):
    return (index // 8, index // 4 % 2, index % 4)


def across_link(value, link):
    axis, distance = link

    def partner(device):
        place = list(grid_place(device))
        place[axis] ^= distance
        return (place[0] * GRID[1] + place[1]) * GRID[2] + place[2]

    size = lax.axis_size("ctx")
    return lax.ppermute(value, "ctx", [(i, partner(i)) for i in range(size)])


def cut(value, axis, start, stop):
    return lax.slice_in_dim(value, start, stop, axis=axis)


def join_halves(mine, theirs, link, place):
    axis, distance = link
    both = [mine, theirs]
    if GRID[axis] == 2 or (distance == 1 and mine.shape[axis] == 1):
        second = place[axis] % 2 == 1
    elif distance == 3:
        second = place[axis] >= 2
    else:
        outer = (place[axis] == 0) | (place[axis] == 3)
        ends, middle = jnp.where(outer, mine, theirs), jnp.where(outer, theirs, mine)
        return jnp.concatenate([cut(ends, axis, 0, 1), middle, cut(ends, axis, 1, 2)], axis=axis)
    return jnp.where(
        second,
        jnp.concatenate(both[::-1], axis=axis),
        jnp.concatenate(both, axis=axis),
    )


def link_of(step, part):
    return LINKS[(step + part) % len(LINKS)]


def link_mask(link):
    axis, distance = link
    return distance * (8, 4, 1)[axis]


def place_masks(part):
    masks = [0]
    for step in range(len(LINKS)):
        masks = masks + [mask ^ link_mask(link_of(step, part)) for mask in masks]
    return masks


def gather_step(parts, step):
    return [
        jnp.concatenate([part, across_link(part, link_of(step, at))])
        for at, part in enumerate(parts)
    ]


def gather_in_place(part, at):
    place = grid_place(lax.axis_index("ctx"))
    part = part[None, None, None]
    for step in range(len(LINKS)):
        link = link_of(step, at)
        part = join_halves(part, across_link(part, link), link, place)
    return part.reshape(-1, part.shape[-1])


def sum_links(pairs, steps):
    for step in steps:
        sums = [
            kept.astype(F32) + across_link(sent, link_of(step, at)).astype(F32)
            for at, (kept, sent) in enumerate(pairs)
        ]
        if not step:
            return [total[0] for total in sums]
        sums = [total.astype(BF16) for total in sums]
        pairs = [(total[: len(total) // 2], total[len(total) // 2 :]) for total in sums]
    return pairs


def across_ep(value, distance):
    return lax.ppermute(value, "ep", [(i, i ^ distance) for i in range(4)])


def gather_ep(rows, axis):
    half = jnp.concatenate([rows, across_ep(rows, 2)], axis=axis)
    return jnp.concatenate([half, across_ep(half, 1)], axis=axis)


def finish_sum(kept, received):
    half = kept + received.astype(F32)
    size = half.shape[1] // 2
    return half[:, :size] + across_ep(half[:, size:].astype(BF16), 2).astype(F32)


def sum_ep(rows, axis, sent_as=BF16):
    size = rows.shape[axis] // 4

    kept, sent = cut(rows, axis, 0, 2 * size), cut(rows, axis, 2 * size, 4 * size)
    half = kept.astype(F32) + across_ep(sent.astype(sent_as), 1).astype(F32)
    kept, sent = cut(half, axis, 0, size), cut(half, axis, size, 2 * size)
    return kept + across_ep(sent.astype(sent_as), 2).astype(F32)


def quad_member(device, size, distance):
    planes, plane = 4, size // 4
    slot, place = device // plane, device % plane
    if distance % 2:
        place = plane - 1 - place
    return (slot ^ distance) % planes * plane + place


def quad_block(ctx, size, distance):
    plane = size // 4
    slot, place = ctx // plane, ctx % plane
    if distance % 2:
        place = plane - 1 - place
    return (slot ^ distance) * plane + place


def across_quad(value, distance):
    size = lax.axis_size("ctx")
    return lax.ppermute(
        value, "ctx", [(i, quad_member(i, size, distance)) for i in range(size)]
    )


def swap_quad(parts):
    return [parts[0]] + [across_quad(parts[distance], distance) for distance in range(1, 4)]


def pick(parts, index):
    return lax.dynamic_index_in_dim(parts, index, 0, keepdims=False)


def rms_scale(values):
    return lax.rsqrt(jnp.mean(values * values, axis=-1, keepdims=True) + EPSILON)


def rope_tables(positions):
    inverse = jnp.exp(
        jnp.arange(HALF, dtype=F32) * (-2.0 * math.log(10000.0) / HEAD_DIM)
    )
    angles = inverse[:, None] * positions.astype(F32)[..., None, :]
    return jnp.cos(angles), jnp.sin(angles)


def rotate(values, cosine, sine):
    first, second = values[..., :HALF, :], values[..., HALF:, :]
    return jnp.concatenate(
        [first * cosine - second * sine, second * cosine + first * sine], axis=-2
    )


def unrotate(values, cosine, sine):
    first, second = values[..., :HALF, :], values[..., HALF:, :]
    return jnp.concatenate(
        [first * cosine + second * sine, second * cosine - first * sine], axis=-2
    )


def widen(heads_ref, side, target_ref, offset):
    target_ref[...] = jnp.zeros_like(target_ref)
    for head in range(GROUP):
        target_ref[offset : offset + HEAD_DIM, head * BLOCK : (head + 1) * BLOCK] = heads_ref[
            side, head
        ]


def allowed_pairs(key_block, query_block, key_segments, query_segments, row_ref, col_ref):
    keys = col_ref[:, 0:1] + key_block * BLOCK
    queries = row_ref[...] + query_block * BLOCK
    return (key_segments == query_segments) & (keys <= queries)


def forward_kernel(
    blocks_ref,
    q_ref,
    kv_ref,
    seg_row_ref,
    seg_col_ref,
    row_ref,
    col_ref,
    o_ref,
    lse_ref,
    q_wide,
    top,
    total,
    acc,
):
    def one_side(side, nothing):
        query_block = blocks_ref[side]
        widen(q_ref, side, q_wide, 0)
        top[...] = jnp.full_like(top, MASKED)
        total[...] = jnp.zeros_like(total)
        acc[...] = jnp.zeros_like(acc)
        query_segments = seg_row_ref[side]
        covered = query_segments == COVERING

        def add(block, scores, scale_by, new_top):
            weights = jnp.exp(scores - scale_by)
            shrink = jnp.exp(top[...] - new_top)
            top[...] = new_top
            total[...] = total[...] * shrink + jnp.sum(weights, axis=0, keepdims=True)
            added = dot_rows(kv_ref[block], weights.astype(BF16))[HEAD_DIM:]
            acc[...] = acc[...] * shrink + added

        def edge(block, column):
            scores = dot(kv_ref[block], q_wide[...])
            allowed = allowed_pairs(
                block, query_block, seg_col_ref[column][:, 0:1], query_segments, row_ref, col_ref
            )
            scores = jnp.where(allowed, scores, MASKED)
            new_top = jnp.maximum(top[...], jnp.max(scores, axis=0, keepdims=True))
            add(block, scores, new_top, new_top)

        def inner(block, carry):
            scores = dot(kv_ref[block], q_wide[...])
            new_top = jnp.maximum(top[...], jnp.max(scores, axis=0, keepdims=True))
            add(
                block,
                scores,
                jnp.where(covered, new_top, -MASKED),
                jnp.where(covered, new_top, top[...]),
            )
            return carry

        def several(turn, carry):
            first = 1 + 4 * turn
            parts = [kv_ref[first + at] for at in range(4)]
            scores = [dot(part, q_wide[...]) for part in parts]
            highest = top[...]
            for score in scores:
                highest = jnp.maximum(highest, jnp.max(score, axis=0, keepdims=True))
            new_top = jnp.where(covered, highest, top[...])
            scale_by = jnp.where(covered, new_top, -MASKED)
            weights = [jnp.exp(score - scale_by) for score in scores]
            shrink = jnp.exp(top[...] - new_top)
            top[...] = new_top
            total[...] = total[...] * shrink + sum(
                jnp.sum(weight, axis=0, keepdims=True) for weight in weights
            )
            added = sum(
                dot_rows(part, weight.astype(BF16))[HEAD_DIM:]
                for part, weight in zip(parts, weights)
            )
            acc[...] = acc[...] * shrink + added
            return carry

        @pl.when(query_block > 0)
        def _():
            edge(0, COMBOS)

        turns = jnp.maximum(query_block - 1, 0) // 4
        lax.fori_loop(0, turns, several, 0)
        lax.fori_loop(1 + 4 * turns, query_block, inner, 0)
        edge(query_block, side)
        lse_ref[side] = top[...] + jnp.log(total[...])
        result = acc[...] / total[...]
        for head in range(GROUP):
            o_ref[side, head] = result[:, head * BLOCK : (head + 1) * BLOCK]
        return nothing

    lax.fori_loop(0, COMBOS, one_side, 0)


def backward_kernel(
    blocks_ref,
    q_ref,
    do_ref,
    kv_ref,
    o_ref,
    lse_ref,
    seg_row_ref,
    seg_col_ref,
    row_ref,
    col_ref,
    cos_ref,
    sin_ref,
    dq_ref,
    dkv_ref,
    q_wide,
    do_wide,
    q_tall,
    do_tall,
    dq_acc,
    dkv_acc,
):
    dkv_acc[...] = jnp.zeros_like(dkv_acc)

    def one_side(side, nothing):
        query_block = blocks_ref[side]
        widen(q_ref, side, q_wide, 0)
        widen(do_ref, side, do_wide, HEAD_DIM)
        for head in range(GROUP):
            at = slice(head * BLOCK, (head + 1) * BLOCK)
            q_tall[at, :] = q_wide[:, at].astype(F32).T.astype(BF16)
            do_tall[at, :] = do_wide[:, at].astype(F32).T.astype(BF16)
        dq_acc[...] = jnp.zeros_like(dq_acc)
        query_segments = seg_row_ref[side]
        lse = lse_ref[side]
        covered_lse = jnp.where(query_segments == COVERING, lse, -MASKED)
        delta = jnp.concatenate(
            [
                jnp.sum(
                    o_ref[side, head] * do_ref[side, head].astype(F32), axis=0, keepdims=True
                )
                for head in range(GROUP)
            ],
            axis=1,
        )

        def add(block, scores, scale_by):
            weights = jnp.exp(scores - scale_by)
            grad_weights = dot(kv_ref[block], do_wide[...])
            grad_scores = (weights * (grad_weights - delta)).astype(BF16)
            dkv_acc[block] += dot(grad_scores, q_tall[...]) + dot(
                weights.astype(BF16), do_tall[...]
            )
            dq_acc[...] += dot_rows(kv_ref[block], grad_scores)[:HEAD_DIM]

        def edge(block, column):
            scores = dot(kv_ref[block], q_wide[...])
            allowed = allowed_pairs(
                block, query_block, seg_col_ref[column][:, 0:1], query_segments, row_ref, col_ref
            )
            add(block, jnp.where(allowed, scores, MASKED), lse)

        def inner(block, carry):
            add(block, dot(kv_ref[block], q_wide[...]), covered_lse)
            return carry

        def several(turn, carry):
            first = 1 + 4 * turn
            parts = [kv_ref[first + at] for at in range(4)]
            scores = [dot(part, q_wide[...]) for part in parts]
            grads = [dot(part, do_wide[...]) for part in parts]
            weights = [jnp.exp(score - covered_lse) for score in scores]
            grads = [
                (weight * (grad - delta)).astype(BF16) for weight, grad in zip(weights, grads)
            ]
            for at in range(4):
                dkv_acc[first + at] += dot(grads[at], q_tall[...]) + dot(
                    weights[at].astype(BF16), do_tall[...]
                )
            dq_acc[...] += sum(
                dot_rows(part, grad)[:HEAD_DIM] for part, grad in zip(parts, grads)
            )
            return carry

        @pl.when(query_block > 0)
        def _():
            edge(0, COMBOS)

        turns = jnp.maximum(query_block - 1, 0) // 4
        lax.fori_loop(0, turns, several, 0)
        lax.fori_loop(1 + 4 * turns, query_block, inner, 0)
        edge(query_block, side)
        for head in range(GROUP):
            at = slice(head * BLOCK, (head + 1) * BLOCK)
            grad = unrotate(dq_acc[:, at], cos_ref[side], sin_ref[side])
            dq_ref[side, head] = (grad * (1.0 / math.sqrt(HEAD_DIM))).astype(BF16)
        return nothing

    lax.fori_loop(0, COMBOS, one_side, 0)
    dkv_ref[...] = dkv_acc[...].astype(BF16)


def experts_kernel(
    places_ref,
    ep_ref,
    tokens_ref,
    cotangent_ref,
    gates_ref,
    *refs,
):
    halves, refs = refs[:8], refs[8:]
    grad_kept, grad_sent, out_kept, out_sent, pre_ref, hidden_ref = refs[:6]
    weights, grad_acc, out_acc, gate_acc, arrived = refs[6:]
    quarter = hidden_ref.shape[2]
    rows = tokens_ref.shape[0]
    block_rows = halves[0].shape[1]
    width = tokens_ref.shape[1]

    def fetch(q):
        for half in range(2):
            source = halves[2 * q + half]
            for at in range(source.shape[0]):
                start = places_ref[q, half * source.shape[0] + at] * block_rows
                start = pl.multiple_of(start, 16)
                pltpu.make_async_copy(
                    source.at[at],
                    weights.at[q % 2, pl.ds(start, block_rows)],
                    arrived.at[q % 2],
                ).start()

    fetch(0)
    gate_acc[...] = jnp.zeros_like(gate_acc)
    for q in range(4):
        if q < 3:
            fetch(q + 1)
        pltpu.make_async_copy(weights.at[q % 2], weights.at[q % 2], arrived.at[q % 2]).wait()
        weights_in = weights[q % 2, :, : 2 * quarter]
        weights_out = weights[q % 2, :, 2 * quarter :]
        grad_hidden = dot(cotangent_ref[...], weights_out)
        pre = dot(tokens_ref[...], weights_in)
        gate_pre, up_pre = pre[:, :quarter], pre[:, quarter:]
        sigmoid = 1.0 / (1.0 + jnp.exp(-gate_pre))
        activated = gate_pre * sigmoid
        hidden = activated * up_pre
        products = grad_hidden * hidden
        tiles = [(tile, (q * quarter // 128 + tile) // 4) for tile in range(quarter // 128)]
        gates = jnp.concatenate(
            [
                jnp.broadcast_to(gates_ref[:, expert : expert + 1], (rows, 128))
                for _, expert in tiles
            ],
            axis=1,
        )
        for tile, expert in tiles:
            gate_acc[expert] += products[:, tile * 128 : (tile + 1) * 128]
        gated_hidden = (gates * hidden).astype(BF16)
        grad_hidden = gates * grad_hidden
        pre_ref[q, :, :quarter] = (
            grad_hidden * up_pre * sigmoid * (1.0 + gate_pre * (1.0 - sigmoid))
        ).astype(BF16)
        pre_ref[q, :, quarter:] = (grad_hidden * activated).astype(BF16)
        hidden_ref[q] = gated_hidden
        grad = dot_columns(pre_ref[q], weights_in)
        out = dot_columns(gated_hidden, weights_out)
        if q == 0:
            grad_acc[...] = grad
            out_acc[...] = out
        elif q < 3:
            grad_acc[...] += grad
            out_acc[...] += out
        else:
            for batch in range(MB):
                kept = slice(batch * BLOCK, batch * BLOCK + BLOCK // 2)
                sent = slice(batch * BLOCK + BLOCK // 2, (batch + 1) * BLOCK)
                grad_kept[batch, :, :width] = grad_acc[kept] + grad[kept]
                grad_sent[batch, :, :width] = (grad_acc[sent] + grad[sent]).astype(BF16)
                out_kept[batch] = out_acc[kept] + out[kept]
                out_sent[batch] = (out_acc[sent] + out[sent]).astype(BF16)
    columns = lax.broadcasted_iota(jnp.int32, (rows, 128), 1) - ep_ref[0] * EXP_DEV
    message = jnp.zeros((rows, 128), F32)
    for expert in range(EXP_DEV):
        total = jnp.sum(gate_acc[expert], axis=1, keepdims=True)
        high = total.astype(BF16).astype(F32)
        message = jnp.where(columns == expert, high, message)
        message = jnp.where(columns == expert + EXPERTS, total - high, message)
    for batch in range(MB):
        start = batch * BLOCK
        grad_kept[batch, :, width:] = message[start : start + BLOCK // 2]
        grad_sent[batch, :, width:] = message[start + BLOCK // 2 : start + BLOCK].astype(BF16)


def expert_grads_kernel(
    places_ref, tokens_ref, cotangent_ref, pre_ref, hidden_ref, kept_ref, sent_ref, scratch
):
    half, block_rows, _ = kept_ref.shape
    planes, quarter = 4, hidden_ref.shape[2]
    rows = tokens_ref.shape[1] // planes
    blocks = rows // block_rows
    for plane in range(planes):
        at = slice(plane * rows, (plane + 1) * rows)
        scratch[:, : 2 * quarter] = dot_rows(tokens_ref[:, at], pre_ref[0]).astype(BF16)
        scratch[:, 2 * quarter :] = dot_rows(cotangent_ref[:, at], hidden_ref[0]).astype(BF16)
        for block in range(blocks):
            place = places_ref[plane * blocks + block]
            value = scratch[block * block_rows : (block + 1) * block_rows, :]

            @pl.when(place < half)
            def _():
                kept_ref[place] = value

            @pl.when(place >= half)
            def _():
                sent_ref[place - half] = value


SMEM_SPEC = pl.BlockSpec(memory_space=pltpu.SMEM)
VMEM_SPEC = pl.BlockSpec(memory_space=pltpu.VMEM)
HEADS_SHAPE = (COMBOS, GROUP, HEAD_DIM, BLOCK)


ANY_SPEC = pl.BlockSpec(memory_space=pl.ANY)


def run_experts(places, ep, tokens, cotangent, gates, halves):
    rows, width = tokens.shape
    _, block_rows, columns = halves[0].shape
    quarter = columns // 3
    kept_rows = (MB, BLOCK // 2)
    return pl.pallas_call(
        experts_kernel,
        out_shape=(
            jax.ShapeDtypeStruct((*kept_rows, width + 128), F32),
            jax.ShapeDtypeStruct((*kept_rows, width + 128), BF16),
            jax.ShapeDtypeStruct((*kept_rows, width), F32),
            jax.ShapeDtypeStruct((*kept_rows, width), BF16),
            jax.ShapeDtypeStruct((4, rows, 2 * quarter), BF16),
            jax.ShapeDtypeStruct((4, rows, quarter), BF16),
        ),
        in_specs=[SMEM_SPEC] * 2 + [VMEM_SPEC] * 3 + [ANY_SPEC] * 8,
        out_specs=(VMEM_SPEC,) * 6,
        scratch_shapes=[
            pltpu.VMEM((2, width, columns), BF16),
            pltpu.VMEM((rows, width), F32),
            pltpu.VMEM((rows, width), F32),
            pltpu.VMEM((EXP_DEV, rows, 128), F32),
            pltpu.SemaphoreType.DMA((2,)),
        ],
        compiler_params=pltpu.CompilerParams(vmem_limit_bytes=50 * 1024 * 1024),
        cost_estimate=pl.CostEstimate(
            flops=16 * rows * width * columns,
            bytes_accessed=30 * 1024 * 1024,
            transcendentals=4 * rows * quarter,
        ),
        name="run_experts",
    )(places, ep, tokens, cotangent, gates, *halves)


def expert_grads(q, places, tokens, cotangent, pre, hidden, block_rows):
    rows, width = tokens.shape
    quarter = hidden.shape[2]
    half = jax.ShapeDtypeStruct((width // block_rows // 2, block_rows, 3 * quarter), BF16)
    whole = pl.BlockSpec((rows, width), lambda i: (0, 0))
    return pl.pallas_call(
        expert_grads_kernel,
        grid=(1,),
        out_shape=(half, half),
        in_specs=[
            SMEM_SPEC,
            whole,
            whole,
            pl.BlockSpec((1, rows, 2 * quarter), lambda i: (q, 0, 0)),
            pl.BlockSpec((1, rows, quarter), lambda i: (q, 0, 0)),
        ],
        out_specs=(pl.BlockSpec(half.shape, lambda i: (0, 0, 0)),) * 2,
        scratch_shapes=[pltpu.VMEM((width // 4, 3 * quarter), BF16)],
        compiler_params=pltpu.CompilerParams(vmem_limit_bytes=40 * 1024 * 1024),
        cost_estimate=pl.CostEstimate(
            flops=6 * rows * width * quarter,
            bytes_accessed=8 * 1024 * 1024,
            transcendentals=0,
        ),
        name="expert_grads",
    )(places, tokens, cotangent, pre, hidden)


def attend(blocks, queries, keys_values, *places):
    steps = 2 * keys_values.shape[0] + 2
    return pl.pallas_call(
        forward_kernel,
        out_shape=(
            jax.ShapeDtypeStruct(HEADS_SHAPE, F32),
            jax.ShapeDtypeStruct((COMBOS, 1, LANES), F32),
        ),
        in_specs=[SMEM_SPEC] + [VMEM_SPEC] * 6,
        out_specs=(VMEM_SPEC, VMEM_SPEC),
        scratch_shapes=[
            pltpu.VMEM((2 * HEAD_DIM, LANES), BF16),
            pltpu.VMEM((1, LANES), F32),
            pltpu.VMEM((1, LANES), F32),
            pltpu.VMEM((HEAD_DIM, LANES), F32),
        ],
        compiler_params=pltpu.CompilerParams(vmem_limit_bytes=32 * 1024 * 1024),
        cost_estimate=pl.CostEstimate(
            flops=steps * 8 * BLOCK * LANES * HEAD_DIM,
            bytes_accessed=4 * 1024 * 1024,
            transcendentals=steps * BLOCK * LANES,
        ),
        name="attend",
    )(blocks, queries, keys_values, *places)


def attend_back(blocks, queries, grads, keys_values, mixed, lse, *places):
    steps = 2 * keys_values.shape[0] + 2
    return pl.pallas_call(
        backward_kernel,
        out_shape=(
            jax.ShapeDtypeStruct(HEADS_SHAPE, BF16),
            jax.ShapeDtypeStruct(keys_values.shape, BF16),
        ),
        in_specs=[SMEM_SPEC] + [VMEM_SPEC] * 11,
        out_specs=(VMEM_SPEC, VMEM_SPEC),
        scratch_shapes=[
            pltpu.VMEM((2 * HEAD_DIM, LANES), BF16),
            pltpu.VMEM((2 * HEAD_DIM, LANES), BF16),
            pltpu.VMEM((LANES, 2 * HEAD_DIM), BF16),
            pltpu.VMEM((LANES, 2 * HEAD_DIM), BF16),
            pltpu.VMEM((HEAD_DIM, LANES), F32),
            pltpu.VMEM(keys_values.shape, F32),
        ],
        compiler_params=pltpu.CompilerParams(vmem_limit_bytes=40 * 1024 * 1024),
        cost_estimate=pl.CostEstimate(
            flops=steps * 20 * BLOCK * LANES * HEAD_DIM,
            bytes_accessed=6 * 1024 * 1024,
            transcendentals=steps * BLOCK * LANES,
        ),
        name="attend_back",
    )(blocks, queries, grads, keys_values, mixed, lse, *places)


def local(
    inputs,
    cotangent,
    segments,
    routes,
    attn_gain,
    w_query,
    key_weight,
    value_weight,
    w_out,
    ffn_gain,
    router,
    w_gate,
    w_up,
    w_down,
):
    ctx_count = lax.axis_size("ctx")
    ctx = lax.axis_index("ctx")
    ep = lax.axis_index("ep")
    slot = ctx // (ctx_count // 4)
    blocks = jnp.stack([quad_block(ctx, ctx_count, distance) for distance in range(4)])
    rows_weight = w_query.shape[0]
    token_rows = inputs.shape[1]
    width = inputs.shape[2]
    hidden_width = w_gate.shape[2]
    width_query = w_query.shape[1]
    width_key = key_weight.shape[1]
    width_joined = width_query + 2 * width_key
    side_start = width_joined
    small_rows = attn_gain.shape[0]
    owners = [ep ^ owner for owner in CHUNK_OWNERS]

    in_width = EXP_DEV * hidden_width
    quarter = in_width // 4
    expert_rows = [
        jnp.concatenate([w_gate[e] for e in range(EXP_DEV)], axis=1),
        jnp.concatenate([w_up[e] for e in range(EXP_DEV)], axis=1),
        jnp.concatenate([w_down[e].T for e in range(EXP_DEV)], axis=1),
    ]
    weight_parts = [
        jnp.concatenate([rows[:, q * quarter : (q + 1) * quarter] for rows in expert_rows], axis=1)
        for q in range(4)
    ]
    expert_ids = jnp.arange(EXPERTS, dtype=jnp.int32)
    chosen_own = jnp.any(routes[..., None] == expert_ids, axis=2).astype(BF16)
    small_own = jnp.concatenate([attn_gain[:, None], ffn_gain[:, None], router], axis=1)
    small_width = small_own.shape[1]
    small_parts = gather_ep(
        jnp.pad(small_own, ((0, 16 - small_rows), (0, 128 - small_width)))[None], 0
    )[:, :small_rows, :small_width]
    natural = [pick(jnp.asarray(CHUNK_OWNERS), ep ^ part) for part in range(4)]
    small_group = jnp.concatenate([pick(small_parts, part) for part in natural])
    chosen = (
        gather_ep(jnp.pad(chosen_own, ((0, 0), (0, 0), (0, 128 - EXPERTS))), 1)[..., :EXPERTS]
        .reshape(MB * BLOCK, EXPERTS)
    ) > 0
    segment_parts = segments.reshape(MB, 4, token_rows).transpose(1, 0, 2)
    segments_here = jnp.stack([pick(segment_parts, owner) for owner in owners], axis=1)
    seg_width = -(-MB * BLOCK // rows_weight)
    seg_part = jnp.pad(
        segments_here.reshape(-1).astype(BF16), (0, seg_width * rows_weight - MB * BLOCK)
    ).reshape(rows_weight, seg_width)
    side_part = jnp.concatenate([small_group, seg_part], axis=1)
    joined_part = jnp.concatenate(
        [
            w_query,
            key_weight,
            value_weight,
            jnp.pad(side_part, ((0, 0), (0, 128 - side_part.shape[1]))),
        ],
        axis=1,
    )
    inputs_all = gather_ep(inputs, 1).reshape(MB * BLOCK, width)
    joined_all = gather_ctx(after(joined_part, inputs_all))
    joined = joined_all[:, :, :width_joined].reshape(width, width_joined)
    side_all = joined_all[:, :, side_start:].reshape(width, 128)
    experts = [after(part, joined_all)[None] for part in weight_parts]
    w_out_all = gather_in_place(after(w_out.T, joined_all), 4)
    for step in range(4):
        experts = gather_step(experts, step)
    expert_halves = [
        half
        for at, part in enumerate(experts)
        for half in (part, across_link(part, link_of(4, at)))
    ]
    masks = jnp.asarray([place_masks(part) for part in range(4)], jnp.int32)
    expert_places = masks ^ ctx
    grad_places = jnp.stack(
        [
            jnp.asarray([place_masks(part).index(mask) for mask in range(ctx_count)], jnp.int32)[
                jnp.arange(ctx_count, dtype=jnp.int32) ^ ctx
            ]
            for part in range(4)
        ]
    )
    gain_one = side_all[:, 0].astype(F32)
    gain_two = side_all[:, 1].astype(F32)
    router_full = side_all[:, 2 : 2 + EXPERTS]
    seg_all = (
        joined_all[:, :, side_start + small_width : side_start + side_part.shape[1]]
        .reshape(ctx_count, -1)[:, : MB * BLOCK]
        .reshape(ctx_count, MB, BLOCK)
        .astype(F32)
    )
    cotangent_all = gather_ep(cotangent, 1).reshape(MB * BLOCK, width)

    offsets = (
        jnp.stack(owners)[:, None] * token_rows + jnp.arange(token_rows, dtype=jnp.int32)
    ).reshape(BLOCK)
    cosines, sines = rope_tables(blocks[:, None] * BLOCK + offsets)
    cosine_both, sine_both = jnp.tile(cosines[0], (1, MB)), jnp.tile(sines[0], (1, MB))

    def by_combo(heads):
        rows = heads.shape[0] // KV_DEV
        parts = heads.reshape(KV_DEV, rows, MB, BLOCK).transpose(2, 0, 1, 3)
        return parts.reshape(COMBOS, rows, BLOCK)

    def from_combos(parts):
        rows = parts.shape[1]
        parts = parts.reshape(MB, KV_DEV, rows, BLOCK).transpose(1, 2, 0, 3)
        return parts.reshape(KV_DEV * rows, MB * BLOCK)

    def to_attention(heads):
        parts = by_combo(heads).reshape(HEADS_SHAPE)
        return jnp.stack(swap_quad([pick(parts, slot ^ distance) for distance in range(4)]))

    def from_attention(parts):
        parts = jnp.stack(swap_quad([parts[distance] for distance in range(4)]))
        parts = jnp.stack([pick(parts, slot ^ combo) for combo in range(COMBOS)])
        return from_combos(parts.reshape(COMBOS, GROUP * HEAD_DIM, BLOCK))

    values = inputs_all.astype(F32)
    scale_one = rms_scale(values)
    normal_one = values * scale_one
    normed = (normal_one * gain_one).astype(BF16)
    projected = jnp.einsum("td,dc->ct", normed, joined, preferred_element_type=F32)

    def turned(start, stop):
        heads = projected[start:stop].reshape(-1, HEAD_DIM, MB * BLOCK)
        return rotate(heads, cosine_both, sine_both).astype(BF16).reshape(-1, MB * BLOCK)

    keys = by_combo(turned(width_query, width_query + width_key))
    key_values = jnp.concatenate(
        [keys, by_combo(projected[width_query + width_key :].astype(BF16))], axis=1
    ).transpose(0, 2, 1)
    sent = jnp.broadcast_to(
        key_values[:, None], (COMBOS, ctx_count // COMBOS, BLOCK, 2 * HEAD_DIM)
    ).reshape(ctx_count, BLOCK, 2 * HEAD_DIM)
    keys_values = lax.all_to_all(sent, "ctx", 0, 0, tiled=True)
    queries = to_attention(turned(0, width_query) * jnp.asarray(1.0 / math.sqrt(HEAD_DIM), BF16))
    seg_here = pick(seg_all.transpose(1, 0, 2), slot // KV_DEV)
    seg_sides = jnp.stack([pick(seg_here, blocks[side]) for side in range(COMBOS)])
    seg_rows = jnp.tile(seg_sides, (1, GROUP))[:, None, :]
    seg_columns = jnp.broadcast_to(
        jnp.concatenate([seg_sides, seg_here[:1]])[:, :, None], (COMBOS + 1, BLOCK, 128)
    )
    offset_row = jnp.tile(offsets, GROUP)[None, :]
    offset_column = jnp.broadcast_to(offsets[:, None], (BLOCK, 128))
    places = (seg_rows, seg_columns, offset_row, offset_column)
    mixed_parts, lse = attend(
        after(blocks, cotangent_all, chosen.astype(F32), *experts), queries, keys_values, *places
    )
    mixed = from_attention(mixed_parts.astype(BF16))

    attn = jnp.einsum("ht,dh->td", mixed, w_out_all, preferred_element_type=F32)
    attn = sum_ep(attn.reshape(MB, BLOCK, width), 1)
    residual = inputs.astype(F32) + attn
    scale_two = rms_scale(residual)
    normal_two = residual * scale_two
    tokens = (normal_two * gain_two).astype(BF16)
    tokens_all = gather_ep(tokens, 1).reshape(MB * BLOCK, width)

    logits = dot(tokens_all, router_full)
    gates = jax.nn.softmax(jnp.where(chosen, logits, MASKED), axis=-1)
    gates_own = gates.reshape(MB, BLOCK, EXPERTS)[:, :token_rows]
    gates_here = lax.dynamic_slice_in_dim(gates, ep * EXP_DEV, EXP_DEV, axis=1)
    grad_kept, grad_sent, out_kept, out_sent, grad_pre, gated_hidden = run_experts(
        expert_places,
        ep.astype(jnp.int32)[None],
        tokens_all,
        cotangent_all,
        jnp.pad(gates_here, ((0, 0), (0, 128 - EXP_DEV))),
        expert_halves,
    )
    received = across_ep(grad_sent, 1)
    message = finish_sum(grad_kept, received)
    grad_places = after(grad_places, received)
    grad_parts = sum_links(
        [
            expert_grads(
                q, grad_places[q], tokens_all, cotangent_all, grad_pre, gated_hidden, rows_weight
            )
            for q in range(4)
        ],
        (4,),
    )
    outputs = (residual + finish_sum(out_kept, across_ep(out_sent, 1))).astype(BF16)

    grad_gates = (
        message[..., width : width + EXPERTS]
        + message[..., width + EXPERTS : width + 2 * EXPERTS]
    )
    grad_logits = (
        gates_own * (grad_gates - jnp.sum(gates_own * grad_gates, axis=-1, keepdims=True))
    ).astype(BF16)
    grad_tokens = message[..., :width] + jnp.einsum(
        "bte,de->btd", grad_logits, router_full, preferred_element_type=F32
    )
    grad_router = jnp.einsum("btd,bte->de", tokens, grad_logits, preferred_element_type=F32)
    grad_gain_two = jnp.sum(grad_tokens * normal_two, axis=(0, 1))
    small_grads = jnp.concatenate([grad_gain_two[:, None], grad_router], axis=1)
    small_high = lax.reduce_precision(small_grads, 8, 7)
    small_count = small_grads.shape[1]
    small_message = (
        jnp.pad(small_high, ((0, 0), (0, 128 - small_count)))
        + jnp.pad(small_grads - small_high, ((0, 0), (small_count, 128 - 2 * small_count)))
    ).astype(BF16)
    scaled = grad_tokens * gain_two
    grad_residual = cotangent.astype(F32) + scale_two * (
        scaled - normal_two * jnp.mean(scaled * normal_two, axis=-1, keepdims=True)
    )
    grad_attn = gather_ep(grad_residual.astype(BF16), 1).reshape(MB * BLOCK, width)
    grad_mixed = jnp.einsum(
        "td,dh->ht", grad_attn, w_out_all, preferred_element_type=F32
    ).astype(BF16)
    grad_mixed = to_attention(grad_mixed)

    grad_out = jnp.einsum(
        "td,ht->dh", grad_attn, mixed, preferred_element_type=F32
    ).astype(BF16)
    side_message = jnp.concatenate([grad_out, small_message], axis=1)
    blocks = after(blocks, outputs, side_message[:, width_query:])
    grad_queries, grad_keys_values = attend_back(
        blocks,
        queries,
        grad_mixed,
        keys_values,
        mixed_parts,
        lse,
        *places,
        cosines,
        sines,
    )
    received = lax.all_to_all(grad_keys_values, "ctx", 0, 0, tiled=True)
    grad_parts = [(after(kept, received), sent) for kept, sent in grad_parts]
    grad_parts = sum_links(grad_parts, (3, 2, 1, 0))
    received = received.astype(F32)
    received = jnp.sum(
        received.reshape(COMBOS, ctx_count // COMBOS, BLOCK, 2 * HEAD_DIM), axis=1
    ).transpose(0, 2, 1)
    grad_query = from_attention(grad_queries)
    grad_key = unrotate(received[:, :HEAD_DIM], cosines[0], sines[0])
    grad_kv = jnp.concatenate(
        [
            from_combos(grad_key.astype(BF16)),
            from_combos(received[:, HEAD_DIM:].astype(BF16)),
        ]
    )
    grad_partial = dot_rows(
        jnp.concatenate([grad_query, grad_kv]), joined.T
    )
    grad_joined = jnp.concatenate([grad_query, grad_kv])
    grad_joined = jnp.einsum("td,ct->dc", normed, grad_joined, preferred_element_type=F32)
    last_message = jnp.concatenate([grad_joined.astype(BF16), side_message], axis=1)
    grad_partial = after(grad_partial, last_message)
    grad_normed = sum_ep(grad_partial.reshape(MB, BLOCK, width), 1)
    values = inputs.astype(F32)
    scale_own = rms_scale(values)
    normal_own = values * scale_own
    scaled = grad_normed * gain_one
    input_grads = (
        grad_residual
        + scale_own
        * (scaled - normal_own * jnp.mean(scaled * normal_own, axis=-1, keepdims=True))
    ).astype(BF16)

    last_sums = sum_ctx(last_message.reshape(ctx_count, rows_weight, last_message.shape[1]))
    grad_joined = last_sums[:, :width_joined]
    small_at = width_joined + width_query
    grad_out = last_sums[:, width_joined:small_at].T
    small_grads = (
        last_sums[:, small_at : small_at + small_count]
        + last_sums[:, small_at + small_count : small_at + 2 * small_count]
    )
    grad_w_query = grad_joined[:, :width_query]
    grad_w_kv = grad_joined[:, width_query:]
    grad_gain_one = jnp.sum(
        grad_joined * joined_part[:, :width_joined].astype(F32), axis=1, keepdims=True
    ) / side_part[:, :1].astype(F32)
    small_grads = jnp.concatenate([grad_gain_one, small_grads], axis=1)
    small_grads = jnp.pad(small_grads, ((0, 0), (0, 128 - 1 - small_count)))
    small_grads = small_grads.reshape(4, small_rows, 128)
    small_grads = jnp.stack([pick(small_grads, owner) for owner in owners])
    small_grads = sum_ep(small_grads, 0, F32)[0, :, : 1 + small_count]
    def by_expert(which):
        at = slice(which * quarter, (which + 1) * quarter)
        grad = jnp.concatenate([part[:, at] for part in grad_parts], axis=1)
        return jnp.stack(
            [grad[:, e * hidden_width : (e + 1) * hidden_width] for e in range(EXP_DEV)]
        )

    return (
        outputs,
        input_grads,
        small_grads[:, 0],
        grad_w_query,
        grad_w_kv[:, :width_key],
        grad_w_kv[:, width_key:],
        grad_out,
        small_grads[:, 1],
        small_grads[:, 2:],
        by_expert(0),
        by_expert(1),
        by_expert(2).transpose(0, 2, 1),
    )


def solution(mesh):
    rows = P(None, ("ctx", "ep"), None)
    shared = P(("ctx", "ep"))
    weight = P("ctx", "ep")
    out_weight = P("ep", "ctx")
    expert = P("ep", "ctx", None)
    down = P("ep", None, "ctx")
    router = P(("ctx", "ep"), None)
    return jax.shard_map(
        local,
        mesh=mesh,
        in_specs=(
            rows,
            rows,
            P(None, "ctx"),
            rows,
            shared,
            weight,
            weight,
            weight,
            out_weight,
            shared,
            router,
            expert,
            expert,
            down,
        ),
        out_specs=(
            rows,
            rows,
            shared,
            weight,
            weight,
            weight,
            out_weight,
            shared,
            router,
            expert,
            expert,
            down,
        ),
        check_vma=False,
    )
```

```python
import math

import jax
import jax.numpy as jnp
from jax import lax
from jax.experimental import pallas as pl
from jax.experimental.pallas import tpu as pltpu
from jax.sharding import PartitionSpec as P

HEAD_DIM = 64
HALF = 32
GROUP = 3
KV_DEV = 2
EXP_DEV = 3
EXPERTS = 12
MB = 2
COMBOS = MB * KV_DEV
BLOCK = 256
LANES = GROUP * BLOCK
COVERING = 4.0
EPSILON = 1e-06
MASKED = -1e30
F32 = jnp.float32
BF16 = jnp.bfloat16
CHUNK_OWNERS = (0, 2, 1, 3)


def dot(left, right):
    return jnp.dot(left, right, preferred_element_type=F32)


def dot_rows(left, right):
    return lax.dot_general(left, right, (((0,), (0,)), ((), ())), preferred_element_type=F32)


def dot_columns(left, right):
    return lax.dot_general(left, right, (((1,), (1,)), ((), ())), preferred_element_type=F32)


def gather_ctx(part):
    copies = jnp.broadcast_to(part[None], (lax.axis_size("ctx"), *part.shape))
    return lax.all_to_all(copies, "ctx", 0, 0, tiled=True)


def sum_ctx(parts):
    return jnp.sum(lax.all_to_all(parts, "ctx", 0, 0, tiled=True).astype(F32), axis=0)


def after(value, *others):
    for other in others:
        first = lax.slice(other, (0,) * other.ndim, (1,) * other.ndim).reshape(())
        value = value + (first * 0).astype(value.dtype)
    return value


LINKS = ((1, 1), (2, 1), (0, 1), (2, 3), (0, 3))
GRID = (4, 2, 4)


def grid_place(index):
    return (index // 8, index // 4 % 2, index % 4)


def across_link(value, link):
    axis, distance = link

    def partner(device):
        place = list(grid_place(device))
        place[axis] ^= distance
        return (place[0] * GRID[1] + place[1]) * GRID[2] + place[2]

    size = lax.axis_size("ctx")
    return lax.ppermute(value, "ctx", [(i, partner(i)) for i in range(size)])


def cut(value, axis, start, stop):
    return lax.slice_in_dim(value, start, stop, axis=axis)


def join_halves(mine, theirs, link, place):
    axis, distance = link
    both = [mine, theirs]
    if GRID[axis] == 2 or (distance == 1 and mine.shape[axis] == 1):
        second = place[axis] % 2 == 1
    elif distance == 3:
        second = place[axis] >= 2
    else:
        outer = (place[axis] == 0) | (place[axis] == 3)
        ends, middle = jnp.where(outer, mine, theirs), jnp.where(outer, theirs, mine)
        return jnp.concatenate([cut(ends, axis, 0, 1), middle, cut(ends, axis, 1, 2)], axis=axis)
    return jnp.where(
        second,
        jnp.concatenate(both[::-1], axis=axis),
        jnp.concatenate(both, axis=axis),
    )


def link_of(step, part):
    return LINKS[(step + part) % len(LINKS)]


def link_mask(link):
    axis, distance = link
    return distance * (8, 4, 1)[axis]


def place_masks(part):
    masks = [0]
    for step in range(len(LINKS)):
        masks = masks + [mask ^ link_mask(link_of(step, part)) for mask in masks]
    return masks


def gather_step(parts, step):
    return [
        jnp.concatenate([part, across_link(part, link_of(step, at))])
        for at, part in enumerate(parts)
    ]


def gather_in_place(part, at):
    place = grid_place(lax.axis_index("ctx"))
    part = part[None, None, None]
    for step in range(len(LINKS)):
        link = link_of(step, at)
        part = join_halves(part, across_link(part, link), link, place)
    return part.reshape(-1, part.shape[-1])


def sum_links(pairs, steps):
    for step in steps:
        sums = [
            kept.astype(F32) + across_link(sent, link_of(step, at)).astype(F32)
            for at, (kept, sent) in enumerate(pairs)
        ]
        if not step:
            return [total[0] for total in sums]
        sums = [total.astype(BF16) for total in sums]
        pairs = [(total[: len(total) // 2], total[len(total) // 2 :]) for total in sums]
    return pairs


def across_ep(value, distance):
    return lax.ppermute(value, "ep", [(i, i ^ distance) for i in range(4)])


def gather_ep(rows, axis):
    half = jnp.concatenate([rows, across_ep(rows, 2)], axis=axis)
    return jnp.concatenate([half, across_ep(half, 1)], axis=axis)


def finish_sum(kept, received):
    half = kept + received.astype(F32)
    size = half.shape[1] // 2
    return half[:, :size] + across_ep(half[:, size:].astype(BF16), 2).astype(F32)


def sum_ep(rows, axis, sent_as=BF16):
    size = rows.shape[axis] // 4

    kept, sent = cut(rows, axis, 0, 2 * size), cut(rows, axis, 2 * size, 4 * size)
    half = kept.astype(F32) + across_ep(sent.astype(sent_as), 1).astype(F32)
    kept, sent = cut(half, axis, 0, size), cut(half, axis, size, 2 * size)
    return kept + across_ep(sent.astype(sent_as), 2).astype(F32)


def quad_member(device, size, distance):
    planes, plane = 4, size // 4
    slot, place = device // plane, device % plane
    if distance % 2:
        place = plane - 1 - place
    return (slot ^ distance) % planes * plane + place


def quad_block(ctx, size, distance):
    plane = size // 4
    slot, place = ctx // plane, ctx % plane
    if distance % 2:
        place = plane - 1 - place
    return (slot ^ distance) * plane + place


def across_quad(value, distance):
    size = lax.axis_size("ctx")
    return lax.ppermute(
        value, "ctx", [(i, quad_member(i, size, distance)) for i in range(size)]
    )


def swap_quad(parts):
    return [parts[0]] + [across_quad(parts[distance], distance) for distance in range(1, 4)]


def pick(parts, index):
    return lax.dynamic_index_in_dim(parts, index, 0, keepdims=False)


def rms_scale(values):
    return lax.rsqrt(jnp.mean(values * values, axis=-1, keepdims=True) + EPSILON)


def rope_tables(positions):
    inverse = jnp.exp(
        jnp.arange(HALF, dtype=F32) * (-2.0 * math.log(10000.0) / HEAD_DIM)
    )
    angles = inverse[:, None] * positions.astype(F32)[..., None, :]
    return jnp.cos(angles), jnp.sin(angles)


def rotate(values, cosine, sine):
    first, second = values[..., :HALF, :], values[..., HALF:, :]
    return jnp.concatenate(
        [first * cosine - second * sine, second * cosine + first * sine], axis=-2
    )


def unrotate(values, cosine, sine):
    first, second = values[..., :HALF, :], values[..., HALF:, :]
    return jnp.concatenate(
        [first * cosine + second * sine, second * cosine - first * sine], axis=-2
    )


def widen(heads_ref, side, target_ref, offset):
    target_ref[...] = jnp.zeros_like(target_ref)
    for head in range(GROUP):
        target_ref[offset : offset + HEAD_DIM, head * BLOCK : (head + 1) * BLOCK] = heads_ref[
            side, head
        ]


def allowed_pairs(key_block, query_block, key_segments, query_segments, row_ref, col_ref):
    keys = col_ref[:, 0:1] + key_block * BLOCK
    queries = row_ref[...] + query_block * BLOCK
    return (key_segments == query_segments) & (keys <= queries)


def forward_kernel(
    blocks_ref,
    q_ref,
    kv_ref,
    seg_row_ref,
    seg_col_ref,
    row_ref,
    col_ref,
    o_ref,
    lse_ref,
    q_wide,
    top,
    total,
    acc,
):
    def one_side(side, nothing):
        query_block = blocks_ref[side]
        widen(q_ref, side, q_wide, 0)
        top[...] = jnp.full_like(top, MASKED)
        total[...] = jnp.zeros_like(total)
        acc[...] = jnp.zeros_like(acc)
        query_segments = seg_row_ref[side]
        covered = query_segments == COVERING

        def add(block, scores, scale_by, new_top):
            weights = jnp.exp(scores - scale_by)
            shrink = jnp.exp(top[...] - new_top)
            top[...] = new_top
            total[...] = total[...] * shrink + jnp.sum(weights, axis=0, keepdims=True)
            added = dot_rows(kv_ref[block], weights.astype(BF16))[HEAD_DIM:]
            acc[...] = acc[...] * shrink + added

        def edge(block, column):
            scores = dot(kv_ref[block], q_wide[...])
            allowed = allowed_pairs(
                block, query_block, seg_col_ref[column][:, 0:1], query_segments, row_ref, col_ref
            )
            scores = jnp.where(allowed, scores, MASKED)
            new_top = jnp.maximum(top[...], jnp.max(scores, axis=0, keepdims=True))
            add(block, scores, new_top, new_top)

        def inner(block, carry):
            scores = dot(kv_ref[block], q_wide[...])
            new_top = jnp.maximum(top[...], jnp.max(scores, axis=0, keepdims=True))
            add(
                block,
                scores,
                jnp.where(covered, new_top, -MASKED),
                jnp.where(covered, new_top, top[...]),
            )
            return carry

        def several(turn, carry):
            first = 1 + 4 * turn
            parts = [kv_ref[first + at] for at in range(4)]
            scores = [dot(part, q_wide[...]) for part in parts]
            highest = top[...]
            for score in scores:
                highest = jnp.maximum(highest, jnp.max(score, axis=0, keepdims=True))
            new_top = jnp.where(covered, highest, top[...])
            scale_by = jnp.where(covered, new_top, -MASKED)
            weights = [jnp.exp(score - scale_by) for score in scores]
            shrink = jnp.exp(top[...] - new_top)
            top[...] = new_top
            total[...] = total[...] * shrink + sum(
                jnp.sum(weight, axis=0, keepdims=True) for weight in weights
            )
            added = sum(
                dot_rows(part, weight.astype(BF16))[HEAD_DIM:]
                for part, weight in zip(parts, weights)
            )
            acc[...] = acc[...] * shrink + added
            return carry

        @pl.when(query_block > 0)
        def _():
            edge(0, COMBOS)

        turns = jnp.maximum(query_block - 1, 0) // 4
        lax.fori_loop(0, turns, several, 0)
        lax.fori_loop(1 + 4 * turns, query_block, inner, 0)
        edge(query_block, side)
        lse_ref[side] = top[...] + jnp.log(total[...])
        result = acc[...] / total[...]
        for head in range(GROUP):
            o_ref[side, head] = result[:, head * BLOCK : (head + 1) * BLOCK]
        return nothing

    lax.fori_loop(0, COMBOS, one_side, 0)


def backward_kernel(
    blocks_ref,
    q_ref,
    do_ref,
    kv_ref,
    o_ref,
    lse_ref,
    seg_row_ref,
    seg_col_ref,
    row_ref,
    col_ref,
    cos_ref,
    sin_ref,
    dq_ref,
    dkv_ref,
    q_wide,
    do_wide,
    q_tall,
    do_tall,
    dq_acc,
    dkv_acc,
):
    dkv_acc[...] = jnp.zeros_like(dkv_acc)

    def one_side(side, nothing):
        query_block = blocks_ref[side]
        widen(q_ref, side, q_wide, 0)
        widen(do_ref, side, do_wide, HEAD_DIM)
        for head in range(GROUP):
            at = slice(head * BLOCK, (head + 1) * BLOCK)
            q_tall[at, :] = q_wide[:, at].astype(F32).T.astype(BF16)
            do_tall[at, :] = do_wide[:, at].astype(F32).T.astype(BF16)
        dq_acc[...] = jnp.zeros_like(dq_acc)
        query_segments = seg_row_ref[side]
        lse = lse_ref[side]
        covered_lse = jnp.where(query_segments == COVERING, lse, -MASKED)
        delta = jnp.concatenate(
            [
                jnp.sum(
                    o_ref[side, head] * do_ref[side, head].astype(F32), axis=0, keepdims=True
                )
                for head in range(GROUP)
            ],
            axis=1,
        )

        def add(block, scores, scale_by):
            weights = jnp.exp(scores - scale_by)
            grad_weights = dot(kv_ref[block], do_wide[...])
            grad_scores = (weights * (grad_weights - delta)).astype(BF16)
            dkv_acc[block] += dot(grad_scores, q_tall[...]) + dot(
                weights.astype(BF16), do_tall[...]
            )
            dq_acc[...] += dot_rows(kv_ref[block], grad_scores)[:HEAD_DIM]

        def edge(block, column):
            scores = dot(kv_ref[block], q_wide[...])
            allowed = allowed_pairs(
                block, query_block, seg_col_ref[column][:, 0:1], query_segments, row_ref, col_ref
            )
            add(block, jnp.where(allowed, scores, MASKED), lse)

        def inner(block, carry):
            add(block, dot(kv_ref[block], q_wide[...]), covered_lse)
            return carry

        def several(turn, carry):
            first = 1 + 4 * turn
            parts = [kv_ref[first + at] for at in range(4)]
            scores = [dot(part, q_wide[...]) for part in parts]
            grads = [dot(part, do_wide[...]) for part in parts]
            weights = [jnp.exp(score - covered_lse) for score in scores]
            grads = [
                (weight * (grad - delta)).astype(BF16) for weight, grad in zip(weights, grads)
            ]
            for at in range(4):
                dkv_acc[first + at] += dot(grads[at], q_tall[...]) + dot(
                    weights[at].astype(BF16), do_tall[...]
                )
            dq_acc[...] += sum(
                dot_rows(part, grad)[:HEAD_DIM] for part, grad in zip(parts, grads)
            )
            return carry

        @pl.when(query_block > 0)
        def _():
            edge(0, COMBOS)

        turns = jnp.maximum(query_block - 1, 0) // 4
        lax.fori_loop(0, turns, several, 0)
        lax.fori_loop(1 + 4 * turns, query_block, inner, 0)
        edge(query_block, side)
        for head in range(GROUP):
            at = slice(head * BLOCK, (head + 1) * BLOCK)
            grad = unrotate(dq_acc[:, at], cos_ref[side], sin_ref[side])
            dq_ref[side, head] = (grad * (1.0 / math.sqrt(HEAD_DIM))).astype(BF16)
        return nothing

    lax.fori_loop(0, COMBOS, one_side, 0)
    dkv_ref[...] = dkv_acc[...].astype(BF16)


def experts_kernel(
    places_ref,
    ep_ref,
    tokens_ref,
    cotangent_ref,
    gates_ref,
    *refs,
):
    halves, refs = refs[:8], refs[8:]
    grad_kept, grad_sent, out_kept, out_sent, pre_ref, hidden_ref = refs[:6]
    weights, grad_acc, out_acc, gate_acc, arrived = refs[6:]
    quarter = hidden_ref.shape[2]
    rows = tokens_ref.shape[0]
    block_rows = halves[0].shape[1]
    width = tokens_ref.shape[1]

    def fetch(q):
        for half in range(2):
            source = halves[2 * q + half]
            for at in range(source.shape[0]):
                start = places_ref[q, half * source.shape[0] + at] * block_rows
                start = pl.multiple_of(start, 16)
                pltpu.make_async_copy(
                    source.at[at],
                    weights.at[q % 2, pl.ds(start, block_rows)],
                    arrived.at[q % 2],
                ).start()

    fetch(0)
    gate_acc[...] = jnp.zeros_like(gate_acc)
    for q in range(4):
        if q < 3:
            fetch(q + 1)
        pltpu.make_async_copy(weights.at[q % 2], weights.at[q % 2], arrived.at[q % 2]).wait()
        weights_in = weights[q % 2, :, : 2 * quarter]
        weights_out = weights[q % 2, :, 2 * quarter :]
        grad_hidden = dot(cotangent_ref[...], weights_out)
        pre = dot(tokens_ref[...], weights_in)
        gate_pre, up_pre = pre[:, :quarter], pre[:, quarter:]
        sigmoid = 1.0 / (1.0 + jnp.exp(-gate_pre))
        activated = gate_pre * sigmoid
        hidden = activated * up_pre
        products = grad_hidden * hidden
        tiles = [(tile, (q * quarter // 128 + tile) // 4) for tile in range(quarter // 128)]
        gates = jnp.concatenate(
            [
                jnp.broadcast_to(gates_ref[:, expert : expert + 1], (rows, 128))
                for _, expert in tiles
            ],
            axis=1,
        )
        for tile, expert in tiles:
            gate_acc[expert] += products[:, tile * 128 : (tile + 1) * 128]
        gated_hidden = (gates * hidden).astype(BF16)
        grad_hidden = gates * grad_hidden
        pre_ref[q, :, :quarter] = (
            grad_hidden * up_pre * sigmoid * (1.0 + gate_pre * (1.0 - sigmoid))
        ).astype(BF16)
        pre_ref[q, :, quarter:] = (grad_hidden * activated).astype(BF16)
        hidden_ref[q] = gated_hidden
        grad = dot_columns(pre_ref[q], weights_in)
        out = dot_columns(gated_hidden, weights_out)
        if q == 0:
            grad_acc[...] = grad
            out_acc[...] = out
        elif q < 3:
            grad_acc[...] += grad
            out_acc[...] += out
        else:
            for batch in range(MB):
                kept = slice(batch * BLOCK, batch * BLOCK + BLOCK // 2)
                sent = slice(batch * BLOCK + BLOCK // 2, (batch + 1) * BLOCK)
                grad_kept[batch, :, :width] = grad_acc[kept] + grad[kept]
                grad_sent[batch, :, :width] = (grad_acc[sent] + grad[sent]).astype(BF16)
                out_kept[batch] = out_acc[kept] + out[kept]
                out_sent[batch] = (out_acc[sent] + out[sent]).astype(BF16)
    columns = lax.broadcasted_iota(jnp.int32, (rows, 128), 1) - ep_ref[0] * EXP_DEV
    message = jnp.zeros((rows, 128), F32)
    for expert in range(EXP_DEV):
        total = jnp.sum(gate_acc[expert], axis=1, keepdims=True)
        high = total.astype(BF16).astype(F32)
        message = jnp.where(columns == expert, high, message)
        message = jnp.where(columns == expert + EXPERTS, total - high, message)
    for batch in range(MB):
        start = batch * BLOCK
        grad_kept[batch, :, width:] = message[start : start + BLOCK // 2]
        grad_sent[batch, :, width:] = message[start + BLOCK // 2 : start + BLOCK].astype(BF16)


def expert_grads_kernel(
    places_ref, tokens_ref, cotangent_ref, pre_ref, hidden_ref, kept_ref, sent_ref, scratch
):
    half, block_rows, _ = kept_ref.shape
    planes, quarter = 4, hidden_ref.shape[2]
    rows = tokens_ref.shape[1] // planes
    blocks = rows // block_rows
    for plane in range(planes):
        at = slice(plane * rows, (plane + 1) * rows)
        scratch[:, : 2 * quarter] = dot_rows(tokens_ref[:, at], pre_ref[0]).astype(BF16)
        scratch[:, 2 * quarter :] = dot_rows(cotangent_ref[:, at], hidden_ref[0]).astype(BF16)
        for block in range(blocks):
            place = places_ref[plane * blocks + block]
            value = scratch[block * block_rows : (block + 1) * block_rows, :]

            @pl.when(place < half)
            def _():
                kept_ref[place] = value

            @pl.when(place >= half)
            def _():
                sent_ref[place - half] = value


SMEM_SPEC = pl.BlockSpec(memory_space=pltpu.SMEM)
VMEM_SPEC = pl.BlockSpec(memory_space=pltpu.VMEM)
HEADS_SHAPE = (COMBOS, GROUP, HEAD_DIM, BLOCK)


ANY_SPEC = pl.BlockSpec(memory_space=pl.ANY)


def run_experts(places, ep, tokens, cotangent, gates, halves):
    rows, width = tokens.shape
    _, block_rows, columns = halves[0].shape
    quarter = columns // 3
    kept_rows = (MB, BLOCK // 2)
    return pl.pallas_call(
        experts_kernel,
        out_shape=(
            jax.ShapeDtypeStruct((*kept_rows, width + 128), F32),
            jax.ShapeDtypeStruct((*kept_rows, width + 128), BF16),
            jax.ShapeDtypeStruct((*kept_rows, width), F32),
            jax.ShapeDtypeStruct((*kept_rows, width), BF16),
            jax.ShapeDtypeStruct((4, rows, 2 * quarter), BF16),
            jax.ShapeDtypeStruct((4, rows, quarter), BF16),
        ),
        in_specs=[SMEM_SPEC] * 2 + [VMEM_SPEC] * 3 + [ANY_SPEC] * 8,
        out_specs=(VMEM_SPEC,) * 6,
        scratch_shapes=[
            pltpu.VMEM((2, width, columns), BF16),
            pltpu.VMEM((rows, width), F32),
            pltpu.VMEM((rows, width), F32),
            pltpu.VMEM((EXP_DEV, rows, 128), F32),
            pltpu.SemaphoreType.DMA((2,)),
        ],
        compiler_params=pltpu.CompilerParams(vmem_limit_bytes=50 * 1024 * 1024),
        cost_estimate=pl.CostEstimate(
            flops=16 * rows * width * columns,
            bytes_accessed=30 * 1024 * 1024,
            transcendentals=4 * rows * quarter,
        ),
        name="run_experts",
    )(places, ep, tokens, cotangent, gates, *halves)


def expert_grads(q, places, tokens, cotangent, pre, hidden, block_rows):
    rows, width = tokens.shape
    quarter = hidden.shape[2]
    half = jax.ShapeDtypeStruct((width // block_rows // 2, block_rows, 3 * quarter), BF16)
    whole = pl.BlockSpec((rows, width), lambda i: (0, 0))
    return pl.pallas_call(
        expert_grads_kernel,
        grid=(1,),
        out_shape=(half, half),
        in_specs=[
            SMEM_SPEC,
            whole,
            whole,
            pl.BlockSpec((1, rows, 2 * quarter), lambda i: (q, 0, 0)),
            pl.BlockSpec((1, rows, quarter), lambda i: (q, 0, 0)),
        ],
        out_specs=(pl.BlockSpec(half.shape, lambda i: (0, 0, 0)),) * 2,
        scratch_shapes=[pltpu.VMEM((width // 4, 3 * quarter), BF16)],
        compiler_params=pltpu.CompilerParams(vmem_limit_bytes=40 * 1024 * 1024),
        cost_estimate=pl.CostEstimate(
            flops=6 * rows * width * quarter,
            bytes_accessed=8 * 1024 * 1024,
            transcendentals=0,
        ),
        name="expert_grads",
    )(places, tokens, cotangent, pre, hidden)


def attend(blocks, queries, keys_values, *places):
    steps = 2 * keys_values.shape[0] + 2
    return pl.pallas_call(
        forward_kernel,
        out_shape=(
            jax.ShapeDtypeStruct(HEADS_SHAPE, F32),
            jax.ShapeDtypeStruct((COMBOS, 1, LANES), F32),
        ),
        in_specs=[SMEM_SPEC] + [VMEM_SPEC] * 6,
        out_specs=(VMEM_SPEC, VMEM_SPEC),
        scratch_shapes=[
            pltpu.VMEM((2 * HEAD_DIM, LANES), BF16),
            pltpu.VMEM((1, LANES), F32),
            pltpu.VMEM((1, LANES), F32),
            pltpu.VMEM((HEAD_DIM, LANES), F32),
        ],
        compiler_params=pltpu.CompilerParams(vmem_limit_bytes=32 * 1024 * 1024),
        cost_estimate=pl.CostEstimate(
            flops=steps * 42 * BLOCK * LANES * HEAD_DIM,
            bytes_accessed=4 * 1024 * 1024,
            transcendentals=steps * BLOCK * LANES,
        ),
        name="attend",
    )(blocks, queries, keys_values, *places)


def attend_back(blocks, queries, grads, keys_values, mixed, lse, *places):
    steps = 2 * keys_values.shape[0] + 2
    return pl.pallas_call(
        backward_kernel,
        out_shape=(
            jax.ShapeDtypeStruct(HEADS_SHAPE, BF16),
            jax.ShapeDtypeStruct(keys_values.shape, BF16),
        ),
        in_specs=[SMEM_SPEC] + [VMEM_SPEC] * 11,
        out_specs=(VMEM_SPEC, VMEM_SPEC),
        scratch_shapes=[
            pltpu.VMEM((2 * HEAD_DIM, LANES), BF16),
            pltpu.VMEM((2 * HEAD_DIM, LANES), BF16),
            pltpu.VMEM((LANES, 2 * HEAD_DIM), BF16),
            pltpu.VMEM((LANES, 2 * HEAD_DIM), BF16),
            pltpu.VMEM((HEAD_DIM, LANES), F32),
            pltpu.VMEM(keys_values.shape, F32),
        ],
        compiler_params=pltpu.CompilerParams(vmem_limit_bytes=40 * 1024 * 1024),
        cost_estimate=pl.CostEstimate(
            flops=steps * 20 * BLOCK * LANES * HEAD_DIM,
            bytes_accessed=6 * 1024 * 1024,
            transcendentals=steps * BLOCK * LANES,
        ),
        name="attend_back",
    )(blocks, queries, grads, keys_values, mixed, lse, *places)


def local(
    inputs,
    cotangent,
    segments,
    routes,
    attn_gain,
    w_query,
    key_weight,
    value_weight,
    w_out,
    ffn_gain,
    router,
    w_gate,
    w_up,
    w_down,
):
    ctx_count = lax.axis_size("ctx")
    ctx = lax.axis_index("ctx")
    ep = lax.axis_index("ep")
    slot = ctx // (ctx_count // 4)
    blocks = jnp.stack([quad_block(ctx, ctx_count, distance) for distance in range(4)])
    rows_weight = w_query.shape[0]
    token_rows = inputs.shape[1]
    width = inputs.shape[2]
    hidden_width = w_gate.shape[2]
    width_query = w_query.shape[1]
    width_key = key_weight.shape[1]
    width_joined = width_query + 2 * width_key
    side_start = width_joined
    small_rows = attn_gain.shape[0]
    owners = [ep ^ owner for owner in CHUNK_OWNERS]

    in_width = EXP_DEV * hidden_width
    quarter = in_width // 4
    expert_rows = [
        jnp.concatenate([w_gate[e] for e in range(EXP_DEV)], axis=1),
        jnp.concatenate([w_up[e] for e in range(EXP_DEV)], axis=1),
        jnp.concatenate([w_down[e].T for e in range(EXP_DEV)], axis=1),
    ]
    weight_parts = [
        jnp.concatenate([rows[:, q * quarter : (q + 1) * quarter] for rows in expert_rows], axis=1)
        for q in range(4)
    ]
    expert_ids = jnp.arange(EXPERTS, dtype=jnp.int32)
    chosen_own = jnp.any(routes[..., None] == expert_ids, axis=2).astype(BF16)
    small_own = jnp.concatenate([attn_gain[:, None], ffn_gain[:, None], router], axis=1)
    small_width = small_own.shape[1]
    small_parts = gather_ep(
        jnp.pad(small_own, ((0, 16 - small_rows), (0, 128 - small_width)))[None], 0
    )[:, :small_rows, :small_width]
    natural = [pick(jnp.asarray(CHUNK_OWNERS), ep ^ part) for part in range(4)]
    small_group = jnp.concatenate([pick(small_parts, part) for part in natural])
    chosen = (
        gather_ep(jnp.pad(chosen_own, ((0, 0), (0, 0), (0, 128 - EXPERTS))), 1)[..., :EXPERTS]
        .reshape(MB * BLOCK, EXPERTS)
    ) > 0
    segment_parts = segments.reshape(MB, 4, token_rows).transpose(1, 0, 2)
    segments_here = jnp.stack([pick(segment_parts, owner) for owner in owners], axis=1)
    seg_width = -(-MB * BLOCK // rows_weight)
    seg_part = jnp.pad(
        segments_here.reshape(-1).astype(BF16), (0, seg_width * rows_weight - MB * BLOCK)
    ).reshape(rows_weight, seg_width)
    side_part = jnp.concatenate([small_group, seg_part], axis=1)
    joined_part = jnp.concatenate(
        [
            w_query,
            key_weight,
            value_weight,
            jnp.pad(side_part, ((0, 0), (0, 128 - side_part.shape[1]))),
        ],
        axis=1,
    )
    inputs_all = gather_ep(inputs, 1).reshape(MB * BLOCK, width)
    joined_all = gather_ctx(after(joined_part, inputs_all))
    joined = joined_all[:, :, :width_joined].reshape(width, width_joined)
    side_all = joined_all[:, :, side_start:].reshape(width, 128)
    experts = [after(part, joined_all)[None] for part in weight_parts]
    w_out_all = gather_in_place(after(w_out.T, joined_all), 4)
    for step in range(4):
        experts = gather_step(experts, step)
    expert_halves = [
        half
        for at, part in enumerate(experts)
        for half in (part, across_link(part, link_of(4, at)))
    ]
    masks = jnp.asarray([place_masks(part) for part in range(4)], jnp.int32)
    expert_places = masks ^ ctx
    grad_places = jnp.stack(
        [
            jnp.asarray([place_masks(part).index(mask) for mask in range(ctx_count)], jnp.int32)[
                jnp.arange(ctx_count, dtype=jnp.int32) ^ ctx
            ]
            for part in range(4)
        ]
    )
    gain_one = side_all[:, 0].astype(F32)
    gain_two = side_all[:, 1].astype(F32)
    router_full = side_all[:, 2 : 2 + EXPERTS]
    seg_all = (
        joined_all[:, :, side_start + small_width : side_start + side_part.shape[1]]
        .reshape(ctx_count, -1)[:, : MB * BLOCK]
        .reshape(ctx_count, MB, BLOCK)
        .astype(F32)
    )
    cotangent_all = gather_ep(cotangent, 1).reshape(MB * BLOCK, width)

    offsets = (
        jnp.stack(owners)[:, None] * token_rows + jnp.arange(token_rows, dtype=jnp.int32)
    ).reshape(BLOCK)
    cosines, sines = rope_tables(blocks[:, None] * BLOCK + offsets)
    cosine_both, sine_both = jnp.tile(cosines[0], (1, MB)), jnp.tile(sines[0], (1, MB))

    def by_combo(heads):
        rows = heads.shape[0] // KV_DEV
        parts = heads.reshape(KV_DEV, rows, MB, BLOCK).transpose(2, 0, 1, 3)
        return parts.reshape(COMBOS, rows, BLOCK)

    def from_combos(parts):
        rows = parts.shape[1]
        parts = parts.reshape(MB, KV_DEV, rows, BLOCK).transpose(1, 2, 0, 3)
        return parts.reshape(KV_DEV * rows, MB * BLOCK)

    def to_attention(heads):
        parts = by_combo(heads).reshape(HEADS_SHAPE)
        return jnp.stack(swap_quad([pick(parts, slot ^ distance) for distance in range(4)]))

    def from_attention(parts):
        parts = jnp.stack(swap_quad([parts[distance] for distance in range(4)]))
        parts = jnp.stack([pick(parts, slot ^ combo) for combo in range(COMBOS)])
        return from_combos(parts.reshape(COMBOS, GROUP * HEAD_DIM, BLOCK))

    values = inputs_all.astype(F32)
    scale_one = rms_scale(values)
    normal_one = values * scale_one
    normed = (normal_one * gain_one).astype(BF16)
    projected = jnp.einsum("td,dc->ct", normed, joined, preferred_element_type=F32)

    def turned(start, stop):
        heads = projected[start:stop].reshape(-1, HEAD_DIM, MB * BLOCK)
        return rotate(heads, cosine_both, sine_both).astype(BF16).reshape(-1, MB * BLOCK)

    keys = by_combo(turned(width_query, width_query + width_key))
    key_values = jnp.concatenate(
        [keys, by_combo(projected[width_query + width_key :].astype(BF16))], axis=1
    ).transpose(0, 2, 1)
    sent = jnp.broadcast_to(
        key_values[:, None], (COMBOS, ctx_count // COMBOS, BLOCK, 2 * HEAD_DIM)
    ).reshape(ctx_count, BLOCK, 2 * HEAD_DIM)
    keys_values = lax.all_to_all(sent, "ctx", 0, 0, tiled=True)
    queries = to_attention(turned(0, width_query) * jnp.asarray(1.0 / math.sqrt(HEAD_DIM), BF16))
    seg_here = pick(seg_all.transpose(1, 0, 2), slot // KV_DEV)
    seg_sides = jnp.stack([pick(seg_here, blocks[side]) for side in range(COMBOS)])
    seg_rows = jnp.tile(seg_sides, (1, GROUP))[:, None, :]
    seg_columns = jnp.broadcast_to(
        jnp.concatenate([seg_sides, seg_here[:1]])[:, :, None], (COMBOS + 1, BLOCK, 128)
    )
    offset_row = jnp.tile(offsets, GROUP)[None, :]
    offset_column = jnp.broadcast_to(offsets[:, None], (BLOCK, 128))
    places = (seg_rows, seg_columns, offset_row, offset_column)
    mixed_parts, lse = attend(
        after(blocks, cotangent_all, chosen.astype(F32), *experts), queries, keys_values, *places
    )
    mixed = from_attention(mixed_parts.astype(BF16))

    attn = jnp.einsum("ht,dh->td", mixed, w_out_all, preferred_element_type=F32)
    attn = sum_ep(attn.reshape(MB, BLOCK, width), 1)
    residual = inputs.astype(F32) + attn
    scale_two = rms_scale(residual)
    normal_two = residual * scale_two
    tokens = (normal_two * gain_two).astype(BF16)
    tokens_all = gather_ep(tokens, 1).reshape(MB * BLOCK, width)

    logits = dot(tokens_all, router_full)
    gates = jax.nn.softmax(jnp.where(chosen, logits, MASKED), axis=-1)
    gates_own = gates.reshape(MB, BLOCK, EXPERTS)[:, :token_rows]
    gates_here = lax.dynamic_slice_in_dim(gates, ep * EXP_DEV, EXP_DEV, axis=1)
    grad_kept, grad_sent, out_kept, out_sent, grad_pre, gated_hidden = run_experts(
        expert_places,
        ep.astype(jnp.int32)[None],
        tokens_all,
        cotangent_all,
        jnp.pad(gates_here, ((0, 0), (0, 128 - EXP_DEV))),
        expert_halves,
    )
    received = across_ep(grad_sent, 1)
    message = finish_sum(grad_kept, received)
    grad_places = after(grad_places, received)
    grad_parts = sum_links(
        [
            expert_grads(
                q, grad_places[q], tokens_all, cotangent_all, grad_pre, gated_hidden, rows_weight
            )
            for q in range(4)
        ],
        (4,),
    )
    outputs = (residual + finish_sum(out_kept, across_ep(out_sent, 1))).astype(BF16)

    grad_gates = (
        message[..., width : width + EXPERTS]
        + message[..., width + EXPERTS : width + 2 * EXPERTS]
    )
    grad_logits = (
        gates_own * (grad_gates - jnp.sum(gates_own * grad_gates, axis=-1, keepdims=True))
    ).astype(BF16)
    grad_tokens = message[..., :width] + jnp.einsum(
        "bte,de->btd", grad_logits, router_full, preferred_element_type=F32
    )
    grad_router = jnp.einsum("btd,bte->de", tokens, grad_logits, preferred_element_type=F32)
    grad_gain_two = jnp.sum(grad_tokens * normal_two, axis=(0, 1))
    small_grads = jnp.concatenate([grad_gain_two[:, None], grad_router], axis=1)
    small_high = lax.reduce_precision(small_grads, 8, 7)
    small_count = small_grads.shape[1]
    small_message = (
        jnp.pad(small_high, ((0, 0), (0, 128 - small_count)))
        + jnp.pad(small_grads - small_high, ((0, 0), (small_count, 128 - 2 * small_count)))
    ).astype(BF16)
    scaled = grad_tokens * gain_two
    grad_residual = cotangent.astype(F32) + scale_two * (
        scaled - normal_two * jnp.mean(scaled * normal_two, axis=-1, keepdims=True)
    )
    grad_attn = gather_ep(grad_residual.astype(BF16), 1).reshape(MB * BLOCK, width)
    grad_mixed = jnp.einsum(
        "td,dh->ht", grad_attn, w_out_all, preferred_element_type=F32
    ).astype(BF16)
    grad_mixed = to_attention(grad_mixed)

    grad_out = jnp.einsum(
        "td,ht->dh", grad_attn, mixed, preferred_element_type=F32
    ).astype(BF16)
    side_message = jnp.concatenate([grad_out, small_message], axis=1)
    blocks = after(blocks, outputs, side_message[:, width_query:])
    grad_queries, grad_keys_values = attend_back(
        blocks,
        queries,
        grad_mixed,
        keys_values,
        mixed_parts,
        lse,
        *places,
        cosines,
        sines,
    )
    received = lax.all_to_all(grad_keys_values, "ctx", 0, 0, tiled=True)
    grad_parts = [(after(kept, received), sent) for kept, sent in grad_parts]
    grad_parts = sum_links(grad_parts, (3, 2, 1, 0))
    received = received.astype(F32)
    received = jnp.sum(
        received.reshape(COMBOS, ctx_count // COMBOS, BLOCK, 2 * HEAD_DIM), axis=1
    ).transpose(0, 2, 1)
    grad_query = from_attention(grad_queries)
    grad_key = unrotate(received[:, :HEAD_DIM], cosines[0], sines[0])
    grad_kv = jnp.concatenate(
        [
            from_combos(grad_key.astype(BF16)),
            from_combos(received[:, HEAD_DIM:].astype(BF16)),
        ]
    )
    grad_partial = dot_rows(
        jnp.concatenate([grad_query, grad_kv]), joined.T
    )
    grad_joined = jnp.concatenate([grad_query, grad_kv])
    grad_joined = jnp.einsum("td,ct->dc", normed, grad_joined, preferred_element_type=F32)
    last_message = jnp.concatenate([grad_joined.astype(BF16), side_message], axis=1)
    grad_partial = after(grad_partial, last_message)
    grad_normed = sum_ep(grad_partial.reshape(MB, BLOCK, width), 1)
    values = inputs.astype(F32)
    scale_own = rms_scale(values)
    normal_own = values * scale_own
    scaled = grad_normed * gain_one
    input_grads = (
        grad_residual
        + scale_own
        * (scaled - normal_own * jnp.mean(scaled * normal_own, axis=-1, keepdims=True))
    ).astype(BF16)

    last_sums = sum_ctx(last_message.reshape(ctx_count, rows_weight, last_message.shape[1]))
    grad_joined = last_sums[:, :width_joined]
    small_at = width_joined + width_query
    grad_out = last_sums[:, width_joined:small_at].T
    small_grads = (
        last_sums[:, small_at : small_at + small_count]
        + last_sums[:, small_at + small_count : small_at + 2 * small_count]
    )
    grad_w_query = grad_joined[:, :width_query]
    grad_w_kv = grad_joined[:, width_query:]
    grad_gain_one = jnp.sum(
        grad_joined * joined_part[:, :width_joined].astype(F32), axis=1, keepdims=True
    ) / side_part[:, :1].astype(F32)
    small_grads = jnp.concatenate([grad_gain_one, small_grads], axis=1)
    small_grads = jnp.pad(small_grads, ((0, 0), (0, 128 - 1 - small_count)))
    small_grads = small_grads.reshape(4, small_rows, 128)
    small_grads = jnp.stack([pick(small_grads, owner) for owner in owners])
    small_grads = sum_ep(small_grads, 0, F32)[0, :, : 1 + small_count]
    def by_expert(which):
        at = slice(which * quarter, (which + 1) * quarter)
        grad = jnp.concatenate([part[:, at] for part in grad_parts], axis=1)
        return jnp.stack(
            [grad[:, e * hidden_width : (e + 1) * hidden_width] for e in range(EXP_DEV)]
        )

    return (
        outputs,
        input_grads,
        small_grads[:, 0],
        grad_w_query,
        grad_w_kv[:, :width_key],
        grad_w_kv[:, width_key:],
        grad_out,
        small_grads[:, 1],
        small_grads[:, 2:],
        by_expert(0),
        by_expert(1),
        by_expert(2).transpose(0, 2, 1),
    )


def solution(mesh):
    rows = P(None, ("ctx", "ep"), None)
    shared = P(("ctx", "ep"))
    weight = P("ctx", "ep")
    out_weight = P("ep", "ctx")
    expert = P("ep", "ctx", None)
    down = P("ep", None, "ctx")
    router = P(("ctx", "ep"), None)
    return jax.shard_map(
        local,
        mesh=mesh,
        in_specs=(
            rows,
            rows,
            P(None, "ctx"),
            rows,
            shared,
            weight,
            weight,
            weight,
            out_weight,
            shared,
            router,
            expert,
            expert,
            down,
        ),
        out_specs=(
            rows,
            rows,
            shared,
            weight,
            weight,
            weight,
            out_weight,
            shared,
            router,
            expert,
            expert,
            down,
        ),
        check_vma=False,
    )
```
